32 devices in a mesh: rep: 16 (over z, x, core), shard: 2 (over y).
Axes of the slice: x: 2, y: 2, z: 4, core: 2. Of those that a mesh axis runs over, the one named last changes fastest.
Arguments:
- tokens: bfloat16 [128, 256, 1024], P(('rep', 'shard')), may hold values from -6 to 6
- cotangent: bfloat16 [128, 256, 1024], P(('rep', 'shard')), may hold values from -6 to 6
- lengths: int32 [32, 3], P(('rep', 'shard')), may hold values from 1 to 4, 8 in all within a row
- adapter_index: int32 [96], P(('rep', 'shard')), may hold values from 0 to 7
- assignment: int32 [256], replicated, may hold values from 0 to 255, each once
- first_gain: float32 [1024], replicated, may hold values from 0.5 to 1.5
- mixer_weight: bfloat16 [1024, 4120], P('shard'), may hold values from -0.1875 to 0.1875
- mixer_down: bfloat16 [128, 1024], P('shard'), may hold values from -0.1875 to 0.1875
- mixer_up: bfloat16 [128, 4120], P('shard'), may hold values from -1.5 to 1.5
- filter_taps: float32 [4, 1792], replicated, may hold values from -3 to 3
- filter_bias: float32 [1792], replicated, may hold values from -3 to 3
- step_bias: float32 [24], replicated, may hold values from -6 to -3
- decay_rate: float32 [24], replicated, may hold values from 0.1 to 8
- skip_gain: float32 [24], replicated, may hold values from 0.5 to 1.5
- state_gain: float32 [1536], replicated, may hold values from 0.5 to 1.5
- merge_weight: bfloat16 [2048, 1024], P('shard'), may hold values from -0.125 to 0.125
- merge_down: bfloat16 [128, 2048], P('shard'), may hold values from -0.125 to 0.125
- merge_up: bfloat16 [128, 1024], P('shard'), may hold values from -1.5 to 1.5
- second_gain: float32 [1024], replicated, may hold values from 0.5 to 1.5
- expand_weight: bfloat16 [1024, 4096], P('shard'), may hold values from -0.1875 to 0.1875
- expand_down: bfloat16 [128, 1024], P('shard'), may hold values from -0.1875 to 0.1875
- expand_up: bfloat16 [128, 4096], P('shard'), may hold values from -1.5 to 1.5
- reduce_weight: bfloat16 [2048, 1024], P('shard'), may hold values from -0.125 to 0.125
- reduce_down: bfloat16 [128, 2048], P('shard'), may hold values from -0.125 to 0.125
- reduce_up: bfloat16 [128, 1024], P('shard'), may hold values from -1.5 to 1.5
Outputs:
- mixed: bfloat16 [128, 256, 1024], P(('rep', 'shard'))
- grad_tokens: float32 [128, 256, 1024], P(('rep', 'shard'))
- grad_mixer_down: float32 [128, 1024], P('shard')
- grad_mixer_up: float32 [128, 4120], P('shard')
- grad_merge_down: float32 [128, 2048], P('shard')
- grad_merge_up: float32 [128, 1024], P('shard')
- grad_expand_down: float32 [128, 1024], P('shard')
- grad_expand_up: float32 [128, 4096], P('shard')
- grad_reduce_down: float32 [128, 2048], P('shard')
- grad_reduce_up: float32 [128, 1024], P('shard')
The draws below stay inside these ranges and needn't reach their ends.
Inputs may be any that keep to these rules, and one draw needn't show every extreme that they name: `lengths`: row b lists, in length units of 128 tokens, the 3 sequences of group b in order; each row sums to 8 and has largest entry 4. `assignment`: a permutation: every length unit of the input appears once.
All inputs are finite; a program needn't handle non-finite values.
Results may differ from the reference program's by a relative error of at most 0.014.
Values may be sent and summed in bfloat16 or wider, within the bound.
No kernel may reach another device: no remote copies, remote signals or barrier semaphores. Data moves between devices by JAX's collectives and lax.ppermute only.
A program may use at most 640 MiB of HBM per device.

```python
import math
import jax
import jax.numpy as jnp
import numpy as np
from jax import lax

D = 1024
FF = 2048
SSM_HEADS = 24
HEAD_P = 64
STATE = 128
ATT_HEADS = 8
KV_HEADS = 2
HEAD_DIM = 64
CONV = 4
RANK = 16
ADAPTERS = 8
SPAN = 128
SEQ_SLOTS = 3
PIECES_DEV = 8
TOK_DEV = 1024
MOST_P = 4
QBLK = 512
DSSM = 1536
XBC = 1792
IN_OUT = 4120
MIX = 2048
ADAPT = 128
BLOCKS = 32
UNITS = 256
NSEQ = 96


def plant(array, rng, smallest, top_value):
    longest = array.shape.index(max(array.shape))
    spots = []
    for shift in (0, 1):
        where = [jax.random.randint(jax.random.fold_in(rng, axis), (), 0, length) for axis, length in enumerate(array.shape)]
        where[longest] = (where[longest] + shift) % array.shape[longest]
        spots.append(tuple(where))
    return array.at[spots[0]].set(smallest).at[spots[1]].set(top_value)


def levels(rng, dims, shards, least, high):
    loudness = 1.0
    for dim, shards_of in shards:
        heights = jax.random.uniform(jax.random.fold_in(jax.random.fold_in(rng, 6), dim), (shards_of,), jnp.float32, least / len(shards), high / len(shards))
        loudness = loudness * jnp.repeat(jnp.exp(heights), dims[dim] // shards_of).reshape((-1,) + (1,) * (len(dims) - 1 - dim))
    return loudness


def length_profile(count, total, reach, slope):
    loads = [(1 << 20) // math.isqrt(standing ** slope) + 1 for standing in range(2, count + 1)]
    rest, given = total - reach - (count - 1), [1] * (count - 1)
    while rest > 0:
        candidates = [i for i in range(count - 1) if given[i] < reach]
        mass, remaining = sum([loads[i] for i in candidates]), rest
        for i in candidates:
            extra = min(reach - given[i], max(1, remaining * loads[i] // mass), rest)
            given[i] = given[i] + extra
            rest = rest - extra
    return np.array([reach] + given)


def uneven_parts(rng, number_of, total, limit, skew):
    if number_of == 2:
        one = jax.random.randint(rng, (), max(1, total - limit), min(limit, total - 1) + 1)
        return jnp.stack([one, total - one])
    sizes = jnp.asarray(length_profile(number_of, total, limit, skew), jnp.int32)
    pairs = (number_of - 1) // 2
    giver, receiver = sizes[1:1 + 2 * pairs:2], sizes[2:2 + 2 * pairs:2]
    room = jnp.minimum(giver - 1, limit - receiver)
    passed = jax.random.randint(jax.random.fold_in(rng, 1), (pairs,), 0, 1 << 20) % (room + 1)
    sizes = sizes.at[1:1 + 2 * pairs:2].set(giver - passed).at[2:2 + 2 * pairs:2].set(receiver + passed)
    return sizes[jax.random.permutation(jax.random.fold_in(rng, 2), number_of)]


def centred(rng, extent, scale, limit, shards=(), kind=jnp.bfloat16):
    drawn = jax.random.normal(rng, extent, jnp.float32) * scale
    if len(shards) > 0:
        drawn = levels(rng, extent, shards, -0.22, 0.18) * drawn
    return jnp.clip(drawn, min=-limit, max=limit).astype(kind)


def setup_inputs(seed: int = 0) -> dict:
    splits = jax.random.split(jax.random.key(seed), 26)
    return {
        "tokens": centred(splits[0], (SPAN, UNITS, D), 1.0, 6.0, ((0, 32),)),
        "cotangent": centred(splits[1], (SPAN, UNITS, D), 1.0, 6.0, ((0, 32),)),
        "lengths": jax.vmap(lambda own: uneven_parts(own, SEQ_SLOTS, PIECES_DEV, MOST_P, 2))(jax.random.split(splits[2], BLOCKS)).reshape((BLOCKS, SEQ_SLOTS)).astype(jnp.int32),
        "adapter_index": plant(jax.random.randint(splits[3], (NSEQ,), 0, ADAPTERS), jax.random.fold_in(splits[3], 1), 0, ADAPTERS - 1).astype(jnp.int32),
        "assignment": jax.random.permutation(splits[4], UNITS).astype(jnp.int32),
        "first_gain": jnp.clip(1.0 + 0.1 * jax.random.normal(splits[5], (D,), jnp.float32), 0.5, 1.5),
        "mixer_weight": centred(splits[6], (D, IN_OUT), D ** -0.5, 0.1875, ((0, 2),)),
        "mixer_down": centred(splits[7], (ADAPT, D), D ** -0.5, 0.1875, ((0, 2),)),
        "mixer_up": centred(splits[8], (ADAPT, IN_OUT), RANK ** -0.5, 1.5, ((0, 2),)),
        "filter_taps": centred(splits[9], (CONV, XBC), CONV ** -0.5, 3.0, (), jnp.float32),
        "filter_bias": centred(splits[10], (XBC,), 0.5, 3.0, (), jnp.float32),
        "step_bias": jnp.clip(jax.random.uniform(splits[11], (SSM_HEADS,), jnp.float32, -6.0, -3.0), -6.0, -3.0),
        "decay_rate": jnp.clip(jnp.exp(jax.random.uniform(splits[12], (SSM_HEADS,), jnp.float32, math.log(0.1), math.log(8.0))), 0.1, 8.0),
        "skip_gain": jnp.clip(jax.random.uniform(splits[13], (SSM_HEADS,), jnp.float32, 0.5, 1.5), 0.5, 1.5),
        "state_gain": jnp.clip(1.0 + 0.1 * jax.random.normal(splits[14], (DSSM,), jnp.float32), 0.5, 1.5),
        "merge_weight": centred(splits[15], (MIX, D), MIX ** -0.5, 0.125, ((0, 2),)),
        "merge_down": centred(splits[16], (ADAPT, MIX), MIX ** -0.5, 0.125, ((0, 2),)),
        "merge_up": centred(splits[17], (ADAPT, D), RANK ** -0.5, 1.5, ((0, 2),)),
        "second_gain": jnp.clip(1.0 + 0.1 * jax.random.normal(splits[18], (D,), jnp.float32), 0.5, 1.5),
        "expand_weight": centred(splits[19], (D, 2 * FF), D ** -0.5, 0.1875, ((0, 2),)),
        "expand_down": centred(splits[20], (ADAPT, D), D ** -0.5, 0.1875, ((0, 2),)),
        "expand_up": centred(splits[21], (ADAPT, 2 * FF), RANK ** -0.5, 1.5, ((0, 2),)),
        "reduce_weight": centred(splits[22], (FF, D), FF ** -0.5, 0.125, ((0, 2),)),
        "reduce_down": centred(splits[23], (ADAPT, FF), FF ** -0.5, 0.125, ((0, 2),)),
        "reduce_up": centred(splits[24], (ADAPT, D), RANK ** -0.5, 1.5, ((0, 2),)),
    }


EPS = 1e-05
ADAPT_SCALE = 0.5
ROPE_BASE = 100000000000.0
NEG = -1e+30
HIGH = lax.Precision.HIGHEST

@jax.custom_vjp
def low(v):
    return lax.optimization_barrier(v.astype(jnp.bfloat16)).astype(jnp.float32)

@jax.custom_vjp
def low_back(v):
    return v

def low_keep(v):
    return (low(v), None)

def low_pass(kept, grad):
    return (grad,)

def back_keep(v):
    return (v, None)

def back_low(kept, grad):
    return (low(grad),)
low.defvjp(low_keep, low_pass)
low_back.defvjp(back_keep, back_low)

def exact_dot(left, right):
    return jnp.dot(left, right, precision=HIGH, preferred_element_type=jnp.float32)

def rms_norm(value, gain):
    return value * lax.rsqrt(lax.optimization_barrier(jnp.mean(value * value, axis=-1, keepdims=True)) + EPS) * gain

def layout(lengths_row, adapter_row, row_count):
    sizes = lengths_row.astype(jnp.int32) * SPAN
    finish = jnp.cumsum(sizes).astype(jnp.int32)
    begin = (finish - sizes).astype(jnp.int32)
    places = jnp.arange(row_count, dtype=jnp.int32)
    member = (places[:, None] >= begin[None, :]) & (places[:, None] < finish[None, :])
    slots = jnp.arange(SEQ_SLOTS, dtype=jnp.int32)
    segment = lax.optimization_barrier(jnp.sum(jnp.where(member, slots[None, :], 0), axis=1)).astype(jnp.int32)
    position = (places - lax.optimization_barrier(jnp.sum(jnp.where(member, begin[None, :], 0), axis=1))).astype(jnp.int32)
    owner = lax.optimization_barrier(jnp.sum(jnp.where(member, adapter_row.astype(jnp.int32)[None, :], 0), axis=1)).astype(jnp.int32)
    columns = jnp.arange(ADAPTERS * RANK, dtype=jnp.int32)
    selector = (columns[None, :] // RANK == owner[:, None]).astype(jnp.float32)
    heads_at = jnp.arange(row_count // SPAN, dtype=jnp.int32) * SPAN
    restart = jnp.any(heads_at[:, None] == begin[None, :], axis=1).astype(jnp.float32)
    lag_masks = jnp.stack([(position >= shift_by).astype(jnp.float32) for shift_by in range(CONV)])
    return (position, segment, selector, restart, lag_masks)

def rotate(flat, position, heads, direction):
    half_dim = HEAD_DIM // 2
    frequency = ROPE_BASE ** (-2.0 * jnp.arange(half_dim, dtype=jnp.float32) / HEAD_DIM)
    angles = position.astype(jnp.float32)[:, None] * frequency[None, :]
    cosine = jnp.cos(angles)[:, None, :]
    sines = direction * jnp.sin(angles)[:, None, :]
    shaped = flat.reshape(flat.shape[0], heads, HEAD_DIM)
    leading = shaped[..., :half_dim]
    trailing = shaped[..., half_dim:]
    turned = jnp.concatenate([leading * cosine - trailing * sines, trailing * cosine + leading * sines], axis=-1)
    return turned.reshape(flat.shape)

def state_scan(inputs_x, vector_b, vector_c, delta, decay_rate, restart):
    row_count = inputs_x.shape[0]
    blocks_n = row_count // SPAN
    inputs_x = inputs_x.reshape(blocks_n, SPAN, SSM_HEADS, HEAD_P)
    vector_b = vector_b.reshape(blocks_n, SPAN, STATE)
    vector_c = vector_c.reshape(blocks_n, SPAN, STATE)
    delta = delta.reshape(blocks_n, SPAN, SSM_HEADS)
    lower = jnp.arange(SPAN)[:, None] >= jnp.arange(SPAN)[None, :]

    def advance(state, pieces):
        block_x, block_b, block_c, block_d, block_r = pieces
        state = state * (1.0 - block_r)
        running = jnp.cumsum(-block_d * decay_rate[None, :], axis=0)
        gaps = jnp.where(lower[:, :, None], running[:, None, :] - running[None, :, :], NEG)
        decays = jnp.exp(gaps)
        inner = jnp.dot(block_c, block_b.T, precision=HIGH)
        weights = inner[:, :, None] * decays * block_d[None, :, :]
        local = jnp.einsum('ijh,jhp->ihp', weights, block_x, precision=HIGH)
        carried = jnp.exp(running)[:, :, None] * jnp.einsum('in,hpn->ihp', block_c, state, precision=HIGH)
        tail = jnp.exp(running[-1][None, :] - running) * block_d
        state = jnp.exp(running[-1])[:, None, None] * state + jnp.einsum('jh,jhp,jn->hpn', tail, block_x, block_b, precision=HIGH)
        return (state, local + carried)
    initial = jnp.zeros((SSM_HEADS, HEAD_P, STATE), jnp.float32)
    _, outputs = lax.scan(advance, initial, (inputs_x, vector_b, vector_c, delta, restart))
    return outputs.reshape(row_count, SSM_HEADS * HEAD_P)

def mamba_mix(gate_part, conv_part, step_part, filter_taps, filter_bias, step_bias, decay_rate, skip_gain, state_gain, lag_masks, restart):
    row_count = conv_part.shape[0]
    summed = filter_bias[None, :]
    for shift_by in range(CONV):
        moved = jnp.pad(conv_part, ((shift_by, 0), (0, 0)))[:row_count]
        summed = summed + filter_taps[shift_by][None, :] * moved * lag_masks[shift_by][:, None]
    convolved = jax.nn.silu(summed)
    inputs_x = convolved[:, :DSSM]
    vector_b = convolved[:, DSSM:DSSM + STATE]
    vector_c = convolved[:, DSSM + STATE:]
    delta = jax.nn.softplus(step_part + step_bias[None, :])
    scanned = state_scan(inputs_x, vector_b, vector_c, delta, decay_rate, restart)
    scanned = scanned + jnp.repeat(skip_gain, HEAD_P)[None, :] * inputs_x
    return rms_norm(scanned * jax.nn.silu(gate_part), state_gain)

def attention(queries, keys_all, values_all, segment, row_count):
    per_group = ATT_HEADS // KV_HEADS
    query_h = queries.reshape(row_count, KV_HEADS, per_group, HEAD_DIM)
    key_h = keys_all.reshape(row_count, KV_HEADS, HEAD_DIM)
    value_h = values_all.reshape(row_count, KV_HEADS, HEAD_DIM)
    places = jnp.arange(row_count, dtype=jnp.int32)
    score_scale = HEAD_DIM ** (-0.5)

    def block(begin_row):
        query_b = lax.dynamic_slice_in_dim(query_h, begin_row, QBLK, 0)
        segment_b = lax.dynamic_slice_in_dim(segment, begin_row, QBLK, 0)
        places_b = begin_row + jnp.arange(QBLK, dtype=jnp.int32)
        raw = jnp.einsum('qhgd,khd->hgqk', query_b, key_h, precision=HIGH) * score_scale
        allowed = (segment_b[:, None] == segment[None, :]) & (places_b[:, None] >= places[None, :])
        scores = low_back(jnp.where(allowed, raw, NEG))
        row_peak = lax.optimization_barrier(jnp.max(scores, axis=-1, keepdims=True))
        raised = jnp.exp(scores - row_peak)
        probability = low(raised / lax.optimization_barrier(jnp.sum(raised, axis=-1, keepdims=True)))
        blended = jnp.einsum('hgqk,khd->qhgd', probability, value_h, precision=HIGH)
        return low_back(blended.reshape(QBLK, ATT_HEADS * HEAD_DIM))
    starts = jnp.arange(row_count // QBLK, dtype=jnp.int32) * QBLK
    return lax.map(jax.checkpoint(block), starts).reshape(row_count, ATT_HEADS * HEAD_DIM)

def project(hidden, weight, lower, upper, selector):
    middle = low_back(low(exact_dot(hidden, lower.T) * selector))
    return low_back(exact_dot(hidden, weight) + ADAPT_SCALE * exact_dot(middle, upper))

def block_forward(values, lengths_row, adapter_row, adapters, frozen):
    mixer_down, mixer_up, merge_down, merge_up, expand_down, expand_up, reduce_down, reduce_up = adapters
    first_gain, mixer_weight, filter_taps, filter_bias, step_bias, decay_rate, skip_gain, state_gain, merge_weight, second_gain, expand_weight, reduce_weight = frozen
    row_count = values.shape[0]
    position, segment, selector, restart, lag_masks = layout(lengths_row, adapter_row, row_count)
    hidden = low(rms_norm(values, first_gain))
    united = project(hidden, mixer_weight, mixer_down, mixer_up, selector)
    offset = DSSM + XBC + SSM_HEADS
    query_width = ATT_HEADS * HEAD_DIM
    key_width = KV_HEADS * HEAD_DIM
    mamba_out = mamba_mix(united[:, :DSSM], united[:, DSSM:DSSM + XBC], united[:, DSSM + XBC:offset], filter_taps, filter_bias, step_bias, decay_rate, skip_gain, state_gain, lag_masks, restart)
    queries = low(rotate(united[:, offset:offset + query_width], position, ATT_HEADS, 1.0))
    keys_low = low(rotate(united[:, offset + query_width:offset + query_width + key_width], position, KV_HEADS, 1.0))
    values_low = low(united[:, offset + query_width + key_width:])
    attended = attention(queries, keys_low, values_low, segment, row_count)
    joined = low(jnp.concatenate([mamba_out, attended], axis=1))
    middle = values + project(joined, merge_weight, merge_down, merge_up, selector)
    second = low(rms_norm(middle, second_gain))
    expanded = project(second, expand_weight, expand_down, expand_up, selector)
    active = low(jax.nn.silu(expanded[:, :FF]) * expanded[:, FF:])
    return middle + project(active, reduce_weight, reduce_down, reduce_up, selector)

def widen(value):
    return value.astype(jnp.float32)

def reference(tokens, cotangent, lengths, adapter_index, assignment, first_gain, mixer_weight, mixer_down, mixer_up, filter_taps, filter_bias, step_bias, decay_rate, skip_gain, state_gain, merge_weight, merge_down, merge_up, second_gain, expand_weight, expand_down, expand_up, reduce_weight, reduce_down, reduce_up):
    frozen = (first_gain, widen(mixer_weight), filter_taps, filter_bias, step_bias, decay_rate, skip_gain, state_gain, widen(merge_weight), second_gain, widen(expand_weight), widen(reduce_weight))
    adapters = (widen(mixer_down), widen(mixer_up), widen(merge_down), widen(merge_up), widen(expand_down), widen(expand_up), widen(reduce_down), widen(reduce_up))
    order = assignment.astype(jnp.int32)
    inverse = jnp.argsort(order).astype(jnp.int32)

    def to_work(value):
        return jnp.take(jnp.transpose(widen(value), (1, 0, 2)), order, axis=0).reshape(BLOCKS, TOK_DEV, D)

    def to_input(value):
        return jnp.transpose(jnp.take(value.reshape(UNITS, SPAN, D), inverse, axis=0), (1, 0, 2))
    inputs = to_work(tokens)
    owners = adapter_index.reshape(BLOCKS, SEQ_SLOTS)

    def forward(values, factors):

        def advance(carry, pieces):
            return (carry, jax.checkpoint(block_forward)(pieces[0], pieces[1], pieces[2], factors, frozen))
        _, outputs = lax.scan(advance, jnp.zeros((), jnp.float32), (values, lengths, owners))
        return outputs
    outputs, backward = jax.vjp(forward, inputs, adapters)
    grad_inputs, grads = backward(to_work(cotangent))
    return (to_input(outputs).astype(jnp.bfloat16), to_input(grad_inputs), grads[0], grads[1], grads[2], grads[3], grads[4], grads[5], grads[6], grads[7])
```

```python
import functools

import jax
import jax.numpy as jnp
from jax import lax
from jax.experimental import pallas as pl
from jax.experimental.pallas import tpu as pltpu
from jax.sharding import PartitionSpec as P

SSM_HEADS = 24
STATE = 128
SPAN = 128
DSSM = 1536
XBC = 1792
CONV = 4
EPS = 1e-05
NEG = -1e30
HIGH = lax.Precision.HIGHEST
F32 = jnp.float32
BF16 = jnp.bfloat16
PAIRS = DSSM // 128
HALO = 8
GATE_C = slice(0, 1536)
QUERY_C = slice(1536, 2048)
KV_C = slice(2048, 2304)
CONV_C = slice(2304, 4096)
STEP_C = slice(4096, 4224)
UNITED = 4224


def dot_nn(a, b):
    return lax.dot_general(a, b, (((1,), (0,)), ((), ())), preferred_element_type=F32)


def dot_nt(a, b):
    return lax.dot_general(a, b, (((1,), (1,)), ((), ())), preferred_element_type=F32)


def dot_exact(a, b):
    return lax.dot_general(
        a, b, (((1,), (0,)), ((), ())), precision=HIGH, preferred_element_type=F32
    )


def split_two(value):
    high = value.astype(BF16)
    return high, (value - high.astype(F32)).astype(BF16)


def spread(value, wide):
    high, rest = split_two(value)
    return dot_nn(jnp.concatenate([high, rest], axis=1), wide)


def gather_heads(value, wide):
    high, rest = split_two(value)
    narrow = wide[:SPAN]
    return dot_nt(high, narrow) + dot_nt(rest, narrow)


def softplus(value):
    return jnp.maximum(value, 0.0) + jnp.log1p(jnp.exp(-jnp.abs(value)))


def sigmoid(value):
    return 1.0 / (1.0 + jnp.exp(-value))


def iota2(dim):
    return lax.broadcasted_iota(jnp.int32, (SPAN, SPAN), dim)


def strip(number):
    return slice(number * 128, (number + 1) * 128)


def filtered(ext, taps_ref, bias_ref, cols):
    total = bias_ref[0:1, cols]
    for lag in range(CONV):
        total = total + taps_ref[lag : lag + 1, cols] * ext[HALO - lag : HALO - lag + SPAN, cols]
    return total


def mamba_forward_kernel(
    restart_ref,
    united_ref,
    attended_ref,
    taps_ref,
    bias_ref,
    step_bias_ref,
    decay_ref,
    skip_ref,
    gain_ref,
    wide_ref,
    out_ref,
    scan_ref,
    start_ref,
    ext,
    state,
    delta_w,
    grow_w,
    tail_w,
    gated_s,
):
    chunk = pl.program_id(0)
    gate_ref = united_ref.at[:, GATE_C]
    conv_ref = united_ref.at[:, CONV_C]
    step_ref = united_ref.at[:, STEP_C]
    out_ref[:, DSSM:] = attended_ref[...]

    @pl.when(restart_ref[chunk] == 1)
    def _():
        state[...] = jnp.zeros_like(state)
        ext[0:HALO, :] = jnp.zeros((HALO, XBC), F32)

    ext[HALO:, :] = conv_ref[...]
    start_ref[0] = state[...]

    step = step_ref[...] + step_bias_ref[0:1, :]
    delta = softplus(step)
    slopes = -delta * decay_ref[0:1, :]
    lower = iota2(0) >= iota2(1)
    running = dot_exact(lower.astype(F32), slopes)
    running_t = running.T
    delta_w[...] = spread(delta, wide_ref[...])
    grow_w[...] = spread(jnp.exp(running), wide_ref[...])
    tail_w[...] = spread(jnp.exp(running[SPAN - 1 :] - running), wide_ref[...])

    def convolved(cols):
        summed = filtered(ext, taps_ref, bias_ref, cols)
        return summed * sigmoid(summed)

    vec_b = convolved(slice(DSSM, DSSM + STATE))
    vec_c = convolved(slice(DSSM + STATE, XBC))
    inner = lax.dot_general(
        vec_c, vec_b, (((1,), (1,)), ((), ())), precision=HIGH, preferred_element_type=F32
    )
    low_c = vec_c.astype(BF16)
    low_bt = vec_b.T.astype(BF16)
    left = iota2(1) < 64
    squares = jnp.zeros((SPAN, SPAN), F32)
    for pair in range(PAIRS):
        cols = strip(pair)
        xs = convolved(cols)
        xd = xs * delta_w[:, cols]
        weights = []
        for head in (2 * pair, 2 * pair + 1):
            gap = running[:, head : head + 1] - running_t[head : head + 1, :]
            decays = jnp.exp(jnp.where(lower, gap, NEG))
            weights.append((inner * decays).astype(BF16))
        stacked = jnp.concatenate(
            [jnp.where(left, xd, 0.0).astype(BF16), jnp.where(left, 0.0, xd).astype(BF16)], axis=0
        )
        local = dot_nn(jnp.concatenate(weights, axis=1), stacked)
        before = state[:, cols]
        scan = local + grow_w[:, cols] * dot_nn(low_c, before.astype(BF16))
        scan_ref[:, cols] = scan
        state[:, cols] = grow_w[SPAN - 1 : SPAN, cols] * before + dot_nn(
            low_bt, (tail_w[:, cols] * xd).astype(BF16)
        )
        gate = gate_ref[:, cols]
        gated = (scan + skip_ref[0:1, cols] * xs) * (gate * sigmoid(gate))
        gated_s[:, cols] = gated
        squares = squares + gated * gated
    scale = lax.rsqrt(jnp.sum(squares, axis=1, keepdims=True) * (1.0 / DSSM) + EPS)
    for pair in range(PAIRS):
        cols = strip(pair)
        out_ref[:, cols] = (gated_s[:, cols] * scale * gain_ref[0:1, cols]).astype(BF16)
    ext[0:HALO, :] = ext[SPAN : SPAN + HALO, :]


def mamba_backward_kernel(
    restart_ref,
    united_ref,
    above_ref,
    scan_ref,
    start_ref,
    grad_ref,
    dquery_ref,
    dkv_ref,
    taps_ref,
    bias_ref,
    step_bias_ref,
    decay_ref,
    skip_ref,
    gain_ref,
    wide_ref,
    dunited_ref,
    ext,
    back,
    dstate,
    delta_w,
    grow_w,
    tail_w,
    xs_s,
    dscan_s,
    sum_s,
    cross_s,
    gain_s,
):
    gate_ref = united_ref.at[:, GATE_C]
    conv_ref = united_ref.at[:, CONV_C]
    step_ref = united_ref.at[:, STEP_C]
    before_ref = above_ref.at[:, CONV_C]
    dgate_ref = dunited_ref.at[:, GATE_C]
    dconv_ref = dunited_ref.at[:, CONV_C]
    dstep_ref = dunited_ref.at[:, STEP_C]
    dunited_ref[:, QUERY_C] = dquery_ref[...]
    dunited_ref[:, KV_C] = dkv_ref[...]
    chunks = pl.num_programs(0)
    chunk = chunks - 1 - pl.program_id(0)
    following = jnp.minimum(chunk + 1, chunks - 1)

    @pl.when((chunk == chunks - 1) | (restart_ref[following] == 1))
    def _():
        dstate[...] = jnp.zeros_like(dstate)
        back[SPAN:, :] = jnp.zeros((HALO, XBC), F32)

    fresh = restart_ref[chunk] == 1
    ext[0:HALO, :] = jnp.where(fresh, 0.0, before_ref[...])
    ext[HALO:, :] = conv_ref[...]

    step = step_ref[...] + step_bias_ref[0:1, :]
    delta = softplus(step)
    slopes = -delta * decay_ref[0:1, :]
    lower = iota2(0) >= iota2(1)
    upper = iota2(0) <= iota2(1)
    running = dot_exact(lower.astype(F32), slopes)
    running_t = running.T
    delta_w[...] = spread(delta, wide_ref[...])
    grow_w[...] = spread(jnp.exp(running), wide_ref[...])
    tail_w[...] = spread(jnp.exp(running[SPAN - 1 :] - running), wide_ref[...])

    def convolved(cols):
        summed = filtered(ext, taps_ref, bias_ref, cols)
        ratio = sigmoid(summed)
        return summed * ratio, ratio * (1.0 + summed * (1.0 - ratio))

    vec_b, slope_b = convolved(slice(DSSM, DSSM + STATE))
    vec_c, slope_c = convolved(slice(DSSM + STATE, XBC))
    inner_t = lax.dot_general(
        vec_b, vec_c, (((1,), (1,)), ((), ())), precision=HIGH, preferred_element_type=F32
    )
    low_b = vec_b.astype(BF16)
    low_c = vec_c.astype(BF16)
    low_ct = vec_c.T.astype(BF16)
    left = iota2(1) < 64

    squares = jnp.zeros((SPAN, SPAN), F32)
    mixed = jnp.zeros((SPAN, SPAN), F32)
    for pair in range(PAIRS):
        cols = strip(pair)
        xs, slope = convolved(cols)
        xs_s[:, cols] = xs
        back[0:SPAN, cols] = slope
        gate = gate_ref[:, cols]
        ratio = sigmoid(gate)
        ssm = scan_ref[:, cols] + skip_ref[0:1, cols] * xs
        gated = ssm * (gate * ratio)
        dmamba = grad_ref[:, cols] * gain_ref[0:1, cols]
        squares = squares + gated * gated
        mixed = mixed + gated * dmamba
    scale = lax.rsqrt(jnp.sum(squares, axis=1, keepdims=True) * (1.0 / DSSM) + EPS)
    pull = scale * scale * scale * (jnp.sum(mixed, axis=1, keepdims=True) * (1.0 / DSSM))

    dinner_t = jnp.zeros((SPAN, SPAN), F32)
    dvec_b = jnp.zeros((SPAN, STATE), F32)
    dvec_c = jnp.zeros((SPAN, STATE), F32)
    for pair in range(PAIRS):
        cols = strip(pair)
        xs = xs_s[:, cols]
        gate = gate_ref[:, cols]
        ratio = sigmoid(gate)
        lit = gate * ratio
        scan = scan_ref[:, cols]
        ssm = scan + skip_ref[0:1, cols] * xs
        gated = ssm * lit
        dgated = scale * (grad_ref[:, cols] * gain_ref[0:1, cols]) - pull * gated
        dgate_ref[:, cols] = (dgated * ssm * (ratio * (1.0 + gate * (1.0 - ratio)))).astype(BF16)
        dscan = dgated * lit
        low_dy = dscan.astype(BF16)
        delta_c = delta_w[:, cols]
        xd = xs * delta_c
        low_xd = xd.astype(BF16)
        xd_both = jnp.concatenate(
            [jnp.where(left, xd, 0.0).astype(BF16), jnp.where(left, 0.0, xd).astype(BF16)], axis=0
        )
        dy_both = jnp.concatenate(
            [jnp.where(left, dscan, 0.0).astype(BF16), jnp.where(left, 0.0, dscan).astype(BF16)],
            axis=0,
        )
        dweights = dot_nt(xd_both, low_dy)
        weights = []
        for place, head in enumerate((2 * pair, 2 * pair + 1)):
            gap = running_t[head : head + 1, :] - running[:, head : head + 1]
            decays = jnp.exp(jnp.where(upper, gap, NEG))
            weights.append((inner_t * decays).astype(BF16))
            dinner_t = dinner_t + dweights[place * SPAN : (place + 1) * SPAN] * decays
        dxd_local = dot_nn(jnp.concatenate(weights, axis=1), dy_both)
        after = dstate[:, cols]
        low_after = after.astype(BF16)
        start = start_ref[0, :, cols]
        tail_c = tail_w[:, cols]
        grow_c = grow_w[:, cols]
        grow_last = grow_w[SPAN - 1 : SPAN, cols]
        dxd_state = tail_c * dot_nn(low_b, low_after)
        dxd = dxd_local + dxd_state
        dvec_b = dvec_b + dot_nt((tail_c * xd).astype(BF16), low_after)
        low_edy = (grow_c * dscan).astype(BF16)
        dvec_c = dvec_c + dot_nt(low_edy, start.astype(BF16))
        dstate[:, cols] = grow_last * after + dot_nn(low_ct, low_edy)
        wide_xd = low_xd.astype(F32)
        sum_s[:, cols] = low_dy.astype(F32) * scan - wide_xd * dxd
        cross_s[:, cols] = xs * dxd
        gain_s[0:8, cols] = jnp.broadcast_to(
            grow_last * jnp.sum(after * start, axis=0, keepdims=True)
            + jnp.sum(wide_xd * dxd_state, axis=0, keepdims=True),
            (8, 128),
        )
        dxs = skip_ref[0:1, cols] * dscan + delta_c * dxd
        back[0:SPAN, cols] = dxs * back[0:SPAN, cols]
    dvec_b = dvec_b + dot_nn(dinner_t.astype(BF16), low_c)
    dvec_c = dvec_c + dot_nn(dinner_t.T.astype(BF16), low_b)
    back[0:SPAN, DSSM : DSSM + STATE] = dvec_b * slope_b
    back[0:SPAN, DSSM + STATE :] = dvec_c * slope_c

    last = (iota2(0) == SPAN - 1).astype(F32)
    drunning = gather_heads(sum_s[...], wide_ref[...]) + last * gather_heads(
        gain_s[...], wide_ref[...]
    )[0:1, :]
    dslopes = dot_exact(upper.astype(F32), drunning)
    ddelta = gather_heads(cross_s[...], wide_ref[...]) - decay_ref[0:1, :] * dslopes
    dstep_ref[...] = (ddelta * sigmoid(step)).astype(BF16)

    for number in range(XBC // 128):
        cols = strip(number)
        total = taps_ref[0:1, cols] * back[0:SPAN, cols]
        for lag in range(1, CONV):
            total = total + taps_ref[lag : lag + 1, cols] * back[lag : lag + SPAN, cols]
        dconv_ref[:, cols] = total.astype(BF16)
    back[SPAN:, :] = back[0:HALO, :]


def spread_matrix():
    rows = jnp.arange(2 * SPAN, dtype=jnp.int32)[:, None] % SPAN
    cols = jnp.arange(DSSM, dtype=jnp.int32)[None, :] // 64
    return (rows == cols).astype(BF16)


def pad_row(value, width):
    return jnp.pad(value, (0, width - value.shape[0]))[None, :]


def fixed(shape):
    return pl.BlockSpec(shape, lambda *_: (0,) * len(shape))


def ssm_params(filter_taps, filter_bias, step_bias, decay_rate, skip_gain, state_gain):
    return (
        filter_taps,
        filter_bias[None, :],
        pad_row(step_bias, SPAN),
        pad_row(decay_rate, SPAN),
        jnp.repeat(skip_gain, 64)[None, :],
        state_gain[None, :],
        spread_matrix(),
    )


PARAM_SPECS = [
    fixed((CONV, XBC)),
    fixed((1, XBC)),
    fixed((1, SPAN)),
    fixed((1, SPAN)),
    fixed((1, DSSM)),
    fixed((1, DSSM)),
    fixed((2 * SPAN, DSSM)),
]


def mamba_forward(united, attended, restart, params):
    rows = united.shape[0]
    chunks = rows // SPAN

    def at(width):
        return pl.BlockSpec((SPAN, width), lambda i, *_: (i, 0))

    wide = pltpu.VMEM((SPAN, DSSM), F32)
    return pl.pallas_call(
        mamba_forward_kernel,
        grid_spec=pltpu.PrefetchScalarGridSpec(
            num_scalar_prefetch=1,
            grid=(chunks,),
            in_specs=[at(UNITED), at(attended.shape[1])] + PARAM_SPECS,
            out_specs=[
                at(DSSM + attended.shape[1]),
                at(DSSM),
                pl.BlockSpec((1, STATE, DSSM), lambda i, *_: (i, 0, 0)),
            ],
            scratch_shapes=[pltpu.VMEM((SPAN + HALO, XBC), F32)] + [wide] * 5,
        ),
        out_shape=[
            jax.ShapeDtypeStruct((rows, DSSM + attended.shape[1]), BF16),
            jax.ShapeDtypeStruct((rows, DSSM), F32),
            jax.ShapeDtypeStruct((chunks, STATE, DSSM), F32),
        ],
        compiler_params=pltpu.CompilerParams(
            vmem_limit_bytes=48 << 20, dimension_semantics=("arbitrary",)
        ),
        cost_estimate=pl.CostEstimate(
            flops=20 * 10**9, bytes_accessed=50 * 10**6, transcendentals=0
        ),
        name="mamba_forward",
    )(restart, united, attended, *params)


def mamba_backward(united, scan, starts, grad, dquery, dkv, restart, params):
    rows = united.shape[0]
    chunks = rows // SPAN

    def at(width):
        return pl.BlockSpec((SPAN, width), lambda i, *_: (chunks - 1 - i, 0))

    wide = pltpu.VMEM((SPAN, DSSM), F32)
    tall = pltpu.VMEM((SPAN + HALO, XBC), F32)
    return pl.pallas_call(
        mamba_backward_kernel,
        grid_spec=pltpu.PrefetchScalarGridSpec(
            num_scalar_prefetch=1,
            grid=(chunks,),
            in_specs=[
                at(UNITED),
                pl.BlockSpec(
                    (HALO, UNITED),
                    lambda i, *_: (jnp.maximum((chunks - 1 - i) * (SPAN // HALO) - 1, 0), 0),
                ),
                at(DSSM),
                pl.BlockSpec((1, STATE, DSSM), lambda i, *_: (chunks - 1 - i, 0, 0)),
                at(DSSM),
                at(dquery.shape[1]),
                at(dkv.shape[1]),
            ]
            + PARAM_SPECS,
            out_specs=[at(UNITED)],
            scratch_shapes=[tall, tall] + [wide] * 8 + [pltpu.VMEM((8, DSSM), F32)],
        ),
        out_shape=[jax.ShapeDtypeStruct((rows, UNITED), BF16)],
        compiler_params=pltpu.CompilerParams(
            vmem_limit_bytes=48 << 20, dimension_semantics=("arbitrary",)
        ),
        cost_estimate=pl.CostEstimate(
            flops=45 * 10**9, bytes_accessed=60 * 10**6, transcendentals=0
        ),
        name="mamba_backward",
    )(restart, united, united, scan, starts, grad, dquery, dkv, *params)[0]


ATT_HEADS = 8
KV_HEADS = 2
HEAD_DIM = 64
MOST_P = 4
QUERY_W = ATT_HEADS * HEAD_DIM
KEY_W = KV_HEADS * HEAD_DIM
ROPE_BASE = 100000000000.0


def lanes_of(shape):
    return lax.broadcasted_iota(jnp.int32, shape, 1)


def turn(value, cosine, sines):
    early = (lanes_of(value.shape) // 32) % 2 == 0
    other = jnp.where(early, pltpu.roll(value, 96, 1), pltpu.roll(value, 32, 1))
    return value * cosine + other * sines


def doubled(value, head):
    left = lanes_of(value.shape) < 64
    moved = pltpu.roll(value, 64, 1)
    return jnp.where(left, value, moved) if head == 0 else jnp.where(left, moved, value)


def parted(value):
    left = lanes_of(value.shape) < 64
    return jnp.concatenate([jnp.where(left, value, 0.0), jnp.where(left, 0.0, value)], axis=0)


def joined_heads(value):
    return jnp.concatenate([value[:, :128], value[:, 128:]], axis=0).T


def causal_tail(scores, blocks):
    keys = lax.broadcasted_iota(jnp.int32, (SPAN, 2 * SPAN), 0)
    asks = lax.broadcasted_iota(jnp.int32, (SPAN, 2 * SPAN), 1) % SPAN
    tail = jnp.where(keys <= asks, scores[(blocks - 1) * SPAN :], NEG)
    if blocks == 1:
        return tail
    return jnp.concatenate([scores[: (blocks - 1) * SPAN], tail], axis=0)


def attend_forward_kernel(
    first_ref, query_ref, kv_ref, cos_ref, sin_ref, out_ref, log_ref, turned_ref, kv_low_ref, keys_s, vals_s
):
    block = pl.program_id(0)
    rows = kv_ref.shape[0]

    @pl.when(block == 0)
    def _():
        keys = turn(kv_ref[:, :KEY_W], cos_ref[...], sin_ref[...]).astype(BF16).astype(F32)
        vals = kv_ref[:, KEY_W:].astype(BF16)
        kv_low_ref[:, :KEY_W] = keys.astype(BF16)
        kv_low_ref[:, KEY_W:] = vals
        for head in range(KV_HEADS):
            keys_s[head] = doubled(keys, head).astype(BF16)
        for number in range(rows // SPAN):
            span = slice(number * SPAN, (number + 1) * SPAN)
            vals_s[:, span] = kv_ref[span, KEY_W:].T.astype(BF16)

    here = pl.ds(pl.multiple_of(block * SPAN, SPAN), SPAN)
    cosine = cos_ref[here, :]
    sines = sin_ref[here, :]
    first = first_ref[block]

    def body(blocks):
        window = pl.ds(pl.multiple_of(first * SPAN, SPAN), blocks * SPAN)
        for pair in range(ATT_HEADS // 2):
            cols = strip(pair)
            group = pair // 2
            turned = turn(query_ref[:, cols], cosine, sines).astype(BF16)
            scaled = turned.astype(F32) * (HEAD_DIM**-0.5)
            turned_ref[:, cols] = scaled.astype(BF16)
            scores = dot_nt(keys_s[group, window, :], parted(scaled).astype(BF16))
            scores = causal_tail(scores, blocks)
            peak = jnp.max(scores, axis=0, keepdims=True)
            raised = jnp.exp(scores - peak)
            total = jnp.sum(raised, axis=0, keepdims=True)
            probability = (raised * (1.0 / total)).astype(BF16)
            vals_t = vals_s[group * HEAD_DIM : (group + 1) * HEAD_DIM, window]
            out_ref[:, cols] = joined_heads(dot_nn(vals_t, probability)).astype(BF16)
            logs = peak + jnp.log(total)
            log_ref[0, 2 * pair : 2 * pair + 1, :] = logs[:, :SPAN]
            log_ref[0, 2 * pair + 1 : 2 * pair + 2, :] = logs[:, SPAN:]

    for blocks in range(1, MOST_P + 1):
        pl.when(block - first == blocks - 1)(functools.partial(body, blocks))


def attend_backward_kernel(
    first_ref,
    turned_ref,
    kv_low_ref,
    grad_ref,
    log_ref,
    cos_ref,
    sin_ref,
    dquery_ref,
    dkv_ref,
    keys_s,
    vals_s,
    keys_t,
    dkeys,
    dvals,
):
    block = pl.program_id(0)
    rows = kv_low_ref.shape[0]

    @pl.when(block == 0)
    def _():
        keys = kv_low_ref[:, :KEY_W].astype(F32)
        vals = kv_low_ref[:, KEY_W:].astype(F32)
        for head in range(KV_HEADS):
            keys_s[head] = doubled(keys, head).astype(BF16)
            vals_s[head] = doubled(vals, head).astype(BF16)
        for number in range(rows // SPAN):
            span = slice(number * SPAN, (number + 1) * SPAN)
            keys_t[:, span] = kv_low_ref[span, :KEY_W].astype(F32).T.astype(BF16)
        dkeys[...] = jnp.zeros_like(dkeys)
        dvals[...] = jnp.zeros_like(dvals)

    here = pl.ds(pl.multiple_of(block * SPAN, SPAN), SPAN)
    cosine = cos_ref[here, :]
    sines = -sin_ref[here, :]
    first = first_ref[block]

    def body(blocks):
        window = pl.ds(pl.multiple_of(first * SPAN, SPAN), blocks * SPAN)
        for pair in range(ATT_HEADS // 2):
            cols = strip(pair)
            group = pair // 2
            asks = parted(turned_ref[:, cols].astype(F32)).astype(BF16)
            grads = parted(grad_ref[:, cols].astype(F32)).astype(BF16)
            scores = causal_tail(dot_nt(keys_s[group, window, :], asks), blocks)
            logs = jnp.concatenate(
                [log_ref[0, 2 * pair : 2 * pair + 1, :], log_ref[0, 2 * pair + 1 : 2 * pair + 2, :]],
                axis=1,
            )
            probability = jnp.exp(scores - logs)
            dprob = dot_nt(vals_s[group, window, :], grads)
            inner = jnp.sum(probability * dprob, axis=0, keepdims=True)
            dscore = (probability * (dprob - inner)).astype(BF16)
            keys_g = keys_t[group * HEAD_DIM : (group + 1) * HEAD_DIM, window]
            dquery = joined_heads(dot_nn(keys_g, dscore)) * (HEAD_DIM**-0.5)
            dquery_ref[:, cols] = turn(dquery, cosine, sines).astype(BF16)
            dkeys[group, window, :] += dot_nn(dscore, asks)
            dvals[group, window, :] += dot_nn(probability.astype(BF16), grads)

    for blocks in range(1, MOST_P + 1):
        pl.when(block - first == blocks - 1)(functools.partial(body, blocks))

    @pl.when(block == pl.num_programs(0) - 1)
    def _():
        left = lanes_of((rows, KEY_W)) < 64

        def folded(total):
            sums = [total[head] + pltpu.roll(total[head], 64, 1) for head in range(KV_HEADS)]
            return jnp.where(left, sums[0], sums[1])

        dkv_ref[:, :KEY_W] = turn(folded(dkeys), cos_ref[...], -sin_ref[...]).astype(BF16)
        dkv_ref[:, KEY_W:] = folded(dvals).astype(BF16)


def rotation_tables(position):
    half = HEAD_DIM // 2
    frequency = ROPE_BASE ** (-2.0 * jnp.arange(half, dtype=F32) / HEAD_DIM)
    angles = position.astype(F32)[:, None] * frequency[None, :]
    cosine, sines = jnp.cos(angles), jnp.sin(angles)
    return (
        jnp.concatenate([cosine] * 4, axis=1),
        jnp.concatenate([-sines, sines, -sines, sines], axis=1),
    )


def attend_forward(united, cosine, sines, first):
    rows = united.shape[0]
    blocks = rows // SPAN
    at = pl.BlockSpec((SPAN, QUERY_W), lambda i, *_: (i, 0))
    query_at = pl.BlockSpec((SPAN, QUERY_W), lambda i, *_: (i, QUERY_C.start // QUERY_W))
    kv_at = pl.BlockSpec((rows, 2 * KEY_W), lambda i, *_: (0, KV_C.start // (2 * KEY_W)))
    return pl.pallas_call(
        attend_forward_kernel,
        grid_spec=pltpu.PrefetchScalarGridSpec(
            num_scalar_prefetch=1,
            grid=(blocks,),
            in_specs=[query_at, kv_at, fixed((rows, 128)), fixed((rows, 128))],
            out_specs=[
                at,
                pl.BlockSpec((1, ATT_HEADS, SPAN), lambda i, *_: (i, 0, 0)),
                at,
                fixed((rows, 2 * KEY_W)),
            ],
            scratch_shapes=[
                pltpu.VMEM((KV_HEADS, rows, 128), BF16),
                pltpu.VMEM((KEY_W, rows), BF16),
            ],
        ),
        out_shape=[
            jax.ShapeDtypeStruct((rows, QUERY_W), BF16),
            jax.ShapeDtypeStruct((blocks, ATT_HEADS, SPAN), F32),
            jax.ShapeDtypeStruct((rows, QUERY_W), BF16),
            jax.ShapeDtypeStruct((rows, 2 * KEY_W), BF16),
        ],
        compiler_params=pltpu.CompilerParams(
            vmem_limit_bytes=48 << 20, dimension_semantics=("arbitrary",)
        ),
        cost_estimate=pl.CostEstimate(
            flops=15 * 10**9, bytes_accessed=6 * 10**6, transcendentals=0
        ),
        name="attend_forward",
    )(first, united, united, cosine, sines)


def attend_backward(turned, kv_low, grad, logs, cosine, sines, first):
    rows = turned.shape[0]
    blocks = rows // SPAN
    at = pl.BlockSpec((SPAN, QUERY_W), lambda i, *_: (i, 0))
    return pl.pallas_call(
        attend_backward_kernel,
        grid_spec=pltpu.PrefetchScalarGridSpec(
            num_scalar_prefetch=1,
            grid=(blocks,),
            in_specs=[
                at,
                fixed((rows, 2 * KEY_W)),
                at,
                pl.BlockSpec((1, ATT_HEADS, SPAN), lambda i, *_: (i, 0, 0)),
                fixed((rows, 128)),
                fixed((rows, 128)),
            ],
            out_specs=[at, fixed((rows, 2 * KEY_W))],
            scratch_shapes=[
                pltpu.VMEM((KV_HEADS, rows, 128), BF16),
                pltpu.VMEM((KV_HEADS, rows, 128), BF16),
                pltpu.VMEM((KEY_W, rows), BF16),
                pltpu.VMEM((KV_HEADS, rows, 128), F32),
                pltpu.VMEM((KV_HEADS, rows, 128), F32),
            ],
        ),
        out_shape=[
            jax.ShapeDtypeStruct((rows, QUERY_W), BF16),
            jax.ShapeDtypeStruct((rows, 2 * KEY_W), BF16),
        ],
        compiler_params=pltpu.CompilerParams(
            vmem_limit_bytes=48 << 20, dimension_semantics=("arbitrary",)
        ),
        cost_estimate=pl.CostEstimate(
            flops=15 * 10**9, bytes_accessed=6 * 10**6, transcendentals=0
        ),
        name="attend_backward",
    )(first, turned, kv_low, grad, logs, cosine, sines)


RANKS = 128
ROW_BLOCK = 256
D = 1024
FF = 2048
MIX = 2048
QUARTERS = 4
ADAPT_SCALE = 0.5
COLUMN_STEP = 512
MIXER = (D, UNITED, 0)
MERGE = (MIX, D, D)
EXPAND = (D, 2 * FF, D + MIX)
REDUCE = (FF, D, 2 * D + MIX)
LOWER_W = 2 * D + MIX + FF
PIECES = 3 + 2 * QUARTERS
COPIES = 3 + 3 * QUARTERS


def weight_scratch(shape):
    return [
        pltpu.VMEM((shape[0], shape[1]), BF16),
        pltpu.VMEM((RANKS, shape[1]), BF16),
        pltpu.VMEM((RANKS, shape[0]), BF16),
        pltpu.SemaphoreType.DMA((COPIES,)),
    ]


def weight_copies(info_ref, shape, pieces, scratch):
    depth, _, column = shape
    own_w, own_u, own_l = pieces[:3]
    sent = pieces[3 : 3 + QUARTERS]
    sent_l = pieces[3 + QUARTERS :]
    weight, upper, lower, sems = scratch
    side = info_ref[0]
    columns = pl.ds(column, depth)

    def rows(start, count):
        return pl.ds(pl.multiple_of(start, 16), count)

    jobs = [
        (own_w, weight.at[rows(side * (depth // 2), depth // 2), :]),
        (own_u, upper.at[rows(side * (RANKS // 2), RANKS // 2), :]),
        (own_l.at[:, columns], lower.at[rows(side * (RANKS // 2), RANKS // 2), :]),
    ]
    part = depth // 8
    for number in range(QUARTERS):
        place = info_ref[1 + number]
        base = (1 - side) * (RANKS // 2) + place * 16
        jobs += [
            (
                sent[number].at[pl.ds(0, part), :],
                weight.at[rows((1 - side) * (depth // 2) + place * part, part), :],
            ),
            (sent[number].at[pl.ds(part, 16), :], upper.at[rows(base, 16), :]),
            (sent_l[number].at[:, columns], lower.at[rows(base, 16), :]),
        ]
    return [pltpu.make_async_copy(src, dst, sems.at[i]) for i, (src, dst) in enumerate(jobs)]


def at_first(action):
    pl.when(pl.program_id(0) == 0)(action)


def start_all(copies):
    for copy in copies:
        copy.start()


def wait_all(copies):
    for copy in copies:
        copy.wait()


def halved(value):
    return (value.astype(F32) * ADAPT_SCALE).astype(BF16)


def masked(value, mask):
    return (value * mask).astype(BF16)


def norm_scale(value):
    return lax.rsqrt(jnp.sum(value * value, axis=1, keepdims=True) * (1.0 / value.shape[1]) + EPS)


def norm_back(grad, value, gain):
    scale = norm_scale(value)
    pulled = grad * gain
    inner = jnp.sum(pulled * value, axis=1, keepdims=True) * (1.0 / value.shape[1])
    return scale * pulled - value * (scale * scale * scale * inner)


def dot_tn(a, b):
    return lax.dot_general(a, b, (((0,), (0,)), ((), ())), preferred_element_type=F32)


def columns_of(width):
    return [slice(at, min(at + COLUMN_STEP, width)) for at in range(0, width, COLUMN_STEP)]


def mixer_forward_kernel(info_ref, x_ref, mask_ref, gain_ref, *rest):
    pieces = rest[:PIECES]
    united_ref, hidden_ref, mid_ref = rest[PIECES : PIECES + 3]
    scratch = rest[PIECES + 3 :]
    weight, upper, lower, _ = scratch
    copies = weight_copies(info_ref, MIXER, pieces, scratch)
    at_first(lambda: start_all(copies))
    value = x_ref[...].astype(F32)
    hidden = (value * norm_scale(value) * gain_ref[0:1, :]).astype(BF16)
    hidden_ref[...] = hidden
    at_first(lambda: wait_all(copies))
    mid = masked(dot_nt(hidden, lower[...]), mask_ref[...].astype(F32))
    mid_ref[...] = mid
    half = halved(mid)
    for cols in columns_of(UNITED):
        united_ref[:, cols] = dot_nn(hidden, weight[:, cols]) + dot_nn(half, upper[:, cols])


def block_forward_kernel(info_ref, joined_ref, x_ref, mask_ref, gain_ref, *rest):
    merge_p, expand_p, reduce_p = (rest[i * PIECES : (i + 1) * PIECES] for i in range(3))
    rest = rest[3 * PIECES :]
    mixed_ref, middle_ref, second_ref, lit_ref, up_ref, mids_ref = rest[:6]
    merge_s, expand_s, reduce_s = (rest[6 + 4 * i : 10 + 4 * i] for i in range(3))
    active_s = rest[18]
    sets = [
        weight_copies(info_ref, shape, pieces, scratch)
        for shape, pieces, scratch in (
            (MERGE, merge_p, merge_s),
            (EXPAND, expand_p, expand_s),
            (REDUCE, reduce_p, reduce_s),
        )
    ]
    at_first(lambda: start_all(sum(sets, [])))
    mask = mask_ref[...].astype(F32)

    at_first(lambda: wait_all(sets[0]))
    weight, upper, lower, _ = merge_s
    joined = joined_ref[...]
    mid = masked(dot_nt(joined, lower[...]), mask)
    mids_ref[:, 0:RANKS] = mid
    middle = x_ref[...].astype(F32) + (
        dot_nn(joined, weight[...]) + dot_nn(halved(mid), upper[...])
    )
    middle_ref[...] = middle
    second = (middle * norm_scale(middle) * gain_ref[0:1, :]).astype(BF16)
    second_ref[...] = second

    at_first(lambda: wait_all(sets[1]))
    weight, upper, lower, _ = expand_s
    mid = masked(dot_nt(second, lower[...]), mask)
    mids_ref[:, RANKS : 2 * RANKS] = mid
    half = halved(mid)
    for cols in columns_of(FF):
        beside = slice(FF + cols.start, FF + cols.stop)
        lit = dot_nn(second, weight[:, cols]) + dot_nn(half, upper[:, cols])
        up = dot_nn(second, weight[:, beside]) + dot_nn(half, upper[:, beside])
        lit_ref[:, cols] = lit
        up_ref[:, cols] = up
        active_s[:, cols] = (lit * sigmoid(lit) * up).astype(BF16)

    at_first(lambda: wait_all(sets[2]))
    weight, upper, lower, _ = reduce_s
    active = active_s[...]
    mid = masked(dot_nt(active, lower[...]), mask)
    mids_ref[:, 2 * RANKS :] = mid
    mixed_ref[...] = (
        middle_ref[...] + (dot_nn(active, weight[...]) + dot_nn(halved(mid), upper[...]))
    ).astype(BF16)


MERGE_L, MERGE_U = slice(0, MIX), slice(MIX, MIX + D)
EXPAND_L, EXPAND_U = slice(MIX + D, MIX + 2 * D), slice(MIX + 2 * D, MIX + 2 * D + 2 * FF)
REDUCE_L = slice(MIX + 2 * D + 2 * FF, MIX + 2 * D + 3 * FF)
REDUCE_U = slice(MIX + 2 * D + 3 * FF, MIX + 3 * D + 3 * FF)
GRADS_W = MIX + 3 * D + 3 * FF


def add_factor_grads(total, lower_cols, upper_cols, grad_mid, hidden, mid, grad):
    gm_t = grad_mid.astype(F32).T.astype(BF16)
    mid_t = (mid.astype(F32) * ADAPT_SCALE).T.astype(BF16)
    total[:, lower_cols] += dot_nn(gm_t, hidden)
    total[:, upper_cols] += dot_nn(mid_t, grad)


def block_backward_kernel(
    info_ref,
    grad_ref,
    joined_ref,
    middle_ref,
    second_ref,
    lit_ref,
    up_ref,
    mids_ref,
    mask_ref,
    gain_ref,
    *rest,
):
    reduce_p, expand_p, merge_p = (rest[i * PIECES : (i + 1) * PIECES] for i in range(3))
    rest = rest[3 * PIECES :]
    dmamba_ref, dattended_ref, dmiddle_ref, grads_ref = rest[:4]
    reduce_s, expand_s, merge_s = (rest[4 + 4 * i : 8 + 4 * i] for i in range(3))
    active_s, dlit_s, total = rest[16:]
    sets = [
        weight_copies(info_ref, shape, pieces, scratch)
        for shape, pieces, scratch in (
            (REDUCE, reduce_p, reduce_s),
            (EXPAND, expand_p, expand_s),
            (MERGE, merge_p, merge_s),
        )
    ]

    def begin():
        for copies in sets:
            start_all(copies)
        total[...] = jnp.zeros_like(total)

    at_first(begin)
    mask = mask_ref[...].astype(F32)

    at_first(lambda: wait_all(sets[0]))
    weight, upper, lower, _ = reduce_s
    grad = grad_ref[...]
    grad_mid = masked(ADAPT_SCALE * dot_nt(grad, upper[...]), mask)
    for cols in columns_of(FF):
        beside = slice(FF + cols.start, FF + cols.stop)
        dactive = dot_nt(grad, weight[cols, :]) + dot_nn(grad_mid, lower[:, cols])
        lit = lit_ref[:, cols]
        up = up_ref[:, cols]
        ratio = sigmoid(lit)
        glow = lit * ratio
        active_s[:, cols] = (glow * up).astype(BF16)
        dlit_s[:, cols] = (dactive * up * (ratio * (1.0 + lit * (1.0 - ratio)))).astype(BF16)
        dlit_s[:, beside] = (dactive * glow).astype(BF16)
    add_factor_grads(
        total, REDUCE_L, REDUCE_U, grad_mid, active_s[...], mids_ref[:, 2 * RANKS :], grad
    )

    at_first(lambda: wait_all(sets[1]))
    weight, upper, lower, _ = expand_s
    dexpanded = dlit_s[...]
    grad_mid = masked(ADAPT_SCALE * dot_nt(dexpanded, upper[...]), mask)
    dsecond = dot_nt(dexpanded, weight[...]) + dot_nn(grad_mid, lower[...])
    dmiddle = grad.astype(F32) + norm_back(dsecond, middle_ref[...], gain_ref[0:1, :])
    dmiddle_ref[...] = dmiddle
    add_factor_grads(
        total,
        EXPAND_L,
        EXPAND_U,
        grad_mid,
        second_ref[...],
        mids_ref[:, RANKS : 2 * RANKS],
        dexpanded,
    )

    at_first(lambda: wait_all(sets[2]))
    weight, upper, lower, _ = merge_s
    grad = dmiddle_ref[...].astype(BF16)
    grad_mid = masked(ADAPT_SCALE * dot_nt(grad, upper[...]), mask)
    for cols in columns_of(MIX):
        djoined = dot_nt(grad, weight[cols, :]) + dot_nn(grad_mid, lower[:, cols])
        if cols.start < DSSM:
            dmamba_ref[:, cols] = djoined
        else:
            dattended_ref[...] = djoined.astype(BF16)
    add_factor_grads(
        total, MERGE_L, MERGE_U, grad_mid, joined_ref[...], mids_ref[:, 0:RANKS], grad
    )

    @pl.when(pl.program_id(0) == pl.num_programs(0) - 1)
    def _():
        grads_ref[...] = total[...].astype(BF16)


MIXER_GRADS_W = D + UNITED + 128


def mixer_backward_kernel(
    info_ref, grad_ref, hidden_ref, x_ref, dmiddle_ref, mid_ref, mask_ref, gain_ref, *rest
):
    pieces = rest[:PIECES]
    out_ref, grads_ref = rest[PIECES : PIECES + 2]
    scratch = rest[PIECES + 2 : PIECES + 6]
    total = rest[PIECES + 6]
    weight, upper, lower, _ = scratch
    copies = weight_copies(info_ref, MIXER, pieces, scratch)

    def begin():
        start_all(copies)
        total[...] = jnp.zeros_like(total)

    at_first(begin)
    at_first(lambda: wait_all(copies))
    grad = grad_ref[...]
    grad_mid = masked(ADAPT_SCALE * dot_nt(grad, upper[...]), mask_ref[...].astype(F32))
    dhidden = dot_nt(grad, weight[...]) + dot_nn(grad_mid, lower[...])
    value = x_ref[...].astype(F32)
    out_ref[...] = (dmiddle_ref[...] + norm_back(dhidden, value, gain_ref[0:1, :])).astype(BF16)
    add_factor_grads(
        total,
        slice(0, D),
        slice(D, D + UNITED),
        grad_mid,
        hidden_ref[...],
        mid_ref[...],
        grad,
    )

    @pl.when(pl.program_id(0) == pl.num_programs(0) - 1)
    def _():
        grads_ref[...] = total[...].astype(BF16)


def row_call(kernel, rows, ins, fixed_ins, raw, outs, fixed_outs, scratch, info, name, flops, moved):
    def at(width):
        return pl.BlockSpec((ROW_BLOCK, width), lambda i, *_: (i, 0))

    return pl.pallas_call(
        kernel,
        grid_spec=pltpu.PrefetchScalarGridSpec(
            num_scalar_prefetch=1,
            grid=(rows // ROW_BLOCK,),
            in_specs=[at(v.shape[1]) for v in ins]
            + [fixed(v.shape) for v in fixed_ins]
            + [pl.BlockSpec(memory_space=pl.ANY)] * len(raw),
            out_specs=[at(width) for width, _ in outs] + [fixed(shape) for shape in fixed_outs],
            scratch_shapes=scratch,
        ),
        out_shape=[jax.ShapeDtypeStruct((rows, width), kind) for width, kind in outs]
        + [jax.ShapeDtypeStruct(shape, BF16) for shape in fixed_outs],
        compiler_params=pltpu.CompilerParams(
            vmem_limit_bytes=60 << 20, dimension_semantics=("arbitrary",)
        ),
        cost_estimate=pl.CostEstimate(flops=flops, bytes_accessed=moved, transcendentals=0),
        name=name,
    )(info, *ins, *fixed_ins, *raw)


def mixer_forward(info, x, mask, gain, pieces):
    rows = x.shape[0]
    return row_call(
        mixer_forward_kernel,
        rows,
        [x, mask],
        [gain[None, :]],
        pieces,
        [(UNITED, F32), (D, BF16), (RANKS, BF16)],
        [],
        weight_scratch(MIXER),
        info,
        "mixer_forward",
        2 * rows * D * UNITED,
        2 * D * UNITED + 4 * rows * UNITED,
    )


def block_forward(info, joined, x, mask, gain, merge_p, expand_p, reduce_p):
    rows = x.shape[0]
    return row_call(
        block_forward_kernel,
        rows,
        [joined, x, mask],
        [gain[None, :]],
        [*merge_p, *expand_p, *reduce_p],
        [(D, BF16), (D, F32), (D, BF16), (FF, F32), (FF, F32), (3 * RANKS, BF16)],
        [],
        weight_scratch(MERGE)
        + weight_scratch(EXPAND)
        + weight_scratch(REDUCE)
        + [pltpu.VMEM((ROW_BLOCK, FF), BF16)],
        info,
        "block_forward",
        2 * rows * D * (MIX + 3 * FF),
        2 * D * (MIX + 3 * FF) + 12 * rows * FF,
    )


def block_backward(info, grad, joined, middle, second, lit, up, mids, mask, gain, merge_p, expand_p, reduce_p):
    rows = grad.shape[0]
    return row_call(
        block_backward_kernel,
        rows,
        [grad, joined, middle, second, lit, up, mids, mask],
        [gain[None, :]],
        [*reduce_p, *expand_p, *merge_p],
        [(DSSM, F32), (MIX - DSSM, BF16), (D, F32)],
        [(RANKS, GRADS_W)],
        weight_scratch(REDUCE)
        + weight_scratch(EXPAND)
        + weight_scratch(MERGE)
        + [
            pltpu.VMEM((ROW_BLOCK, FF), BF16),
            pltpu.VMEM((ROW_BLOCK, 2 * FF), BF16),
            pltpu.VMEM((RANKS, GRADS_W), F32),
        ],
        info,
        "block_backward",
        2 * rows * D * (MIX + 3 * FF),
        2 * D * (MIX + 3 * FF) + 12 * rows * FF,
    )


def mixer_backward(info, grad, hidden, x, dmiddle, mid, mask, gain, pieces):
    rows = x.shape[0]
    return row_call(
        mixer_backward_kernel,
        rows,
        [grad, hidden, x, dmiddle, mid, mask],
        [gain[None, :]],
        pieces,
        [(D, BF16)],
        [(RANKS, MIXER_GRADS_W)],
        weight_scratch(MIXER) + [pltpu.VMEM((RANKS, MIXER_GRADS_W), F32)],
        info,
        "mixer_backward",
        2 * rows * D * UNITED,
        2 * D * UNITED + 8 * rows * D,
    )


SEQ_SLOTS = 3
RANK = 16
STEP_W = 24


def swap_pairs(count, bit):
    return [(i, i ^ bit) for i in range(count)]


def send_quarter(weight, upper, quarter):
    part, own = weight.shape[0] // QUARTERS, upper.shape[0] // QUARTERS
    return jnp.concatenate(
        [
            lax.dynamic_slice_in_dim(weight, quarter * part, part, 0),
            lax.dynamic_slice_in_dim(upper, quarter * own, own, 0),
        ],
        axis=0,
    )


def across(value):
    return lax.ppermute(value, "shard", swap_pairs(2, 1))


def beside(value, bit):
    return lax.ppermute(value, "rep", swap_pairs(lax.axis_size("rep"), bit))


def spread_quarter(first):
    second = beside(first, 2)
    return (first, second, beside(first, 1), beside(second, 1))


def aligned_columns(value):
    gate, conv = value[:, :DSSM], value[:, DSSM : DSSM + XBC]
    step = value[:, DSSM + XBC : DSSM + XBC + STEP_W]
    attention = value[:, DSSM + XBC + STEP_W :]
    padding = jnp.zeros((value.shape[0], SPAN - STEP_W), value.dtype)
    return jnp.concatenate([gate, attention, conv, step, padding], axis=1)


def given_columns(value):
    conv_at = CONV_C.start
    return jnp.concatenate(
        [
            value[:, :DSSM],
            value[:, conv_at : conv_at + XBC],
            value[:, STEP_C.start : STEP_C.start + STEP_W],
            value[:, DSSM:conv_at],
        ],
        axis=1,
    )


def after(value, *others):
    return lax.optimization_barrier((value, *others))[0]


def reduce_factors(grads):
    rows, width = grads.shape
    half, mine = width // 2, rows // 2
    rep = lax.axis_index("rep")
    side = lax.axis_index("shard")
    core = rep % 2
    count = lax.axis_size("rep") // 2
    groups = [[2 * i + place for i in range(count)] for place in range(2)]
    kept = lax.dynamic_slice_in_dim(grads, core * half, half, 1)
    sent = lax.dynamic_slice_in_dim(grads, (1 - core) * half, half, 1)
    total = kept.astype(F32) + beside(sent, 1).astype(F32)
    kept = lax.dynamic_slice_in_dim(total, side * mine, mine, 0)
    sent = lax.dynamic_slice_in_dim(total, (1 - side) * mine, mine, 0).astype(BF16)
    total = (kept + across(sent).astype(F32)).astype(BF16)
    parts = lax.all_to_all(
        total.reshape(count, mine // count, half),
        "rep",
        split_axis=0,
        concat_axis=0,
        axis_index_groups=groups,
        tiled=True,
    )
    own = jnp.sum(parts.astype(F32), axis=0, keepdims=True).astype(BF16)
    whole = lax.all_to_all(
        jnp.broadcast_to(own, (count, *own.shape[1:])),
        "rep",
        split_axis=0,
        concat_axis=0,
        axis_index_groups=groups,
        tiled=True,
    ).reshape(mine, half)
    other = beside(whole, 1)
    return jnp.where(
        core == 0,
        jnp.concatenate([whole, other], axis=1),
        jnp.concatenate([other, whole], axis=1),
    ).astype(F32)


def row_orders(assignment, stripe, groups):
    units = assignment.shape[0]
    per = units // groups
    total = stripe * units
    sending = jnp.arange(total, dtype=jnp.int32)
    group, row, piece = sending // (stripe * per), sending // per % stripe, sending % per
    source = row * units + jnp.take(assignment, group * per + piece)
    columns = jnp.arange(total, dtype=jnp.int32)
    pick = (source[:, None] == columns[None, :]).astype(BF16)
    working = jnp.arange(total, dtype=jnp.int32)
    piece, group, row = working // (groups * stripe), working // stripe % groups, working % stripe
    received = (group * stripe + row) * per + piece
    place = (received[:, None] == columns[None, :]).astype(BF16)
    return pick, place


def exchange(value):
    return lax.all_to_all(value, ("rep", "shard"), split_axis=0, concat_axis=0, tiled=True)


def on_device(
    tokens,
    cotangent,
    lengths,
    adapter_index,
    assignment,
    first_gain,
    mixer_weight,
    mixer_down,
    mixer_up,
    filter_taps,
    filter_bias,
    step_bias,
    decay_rate,
    skip_gain,
    state_gain,
    merge_weight,
    merge_down,
    merge_up,
    second_gain,
    expand_weight,
    expand_down,
    expand_up,
    reduce_weight,
    reduce_down,
    reduce_up,
):
    stripe, units, width = tokens.shape
    groups = lax.axis_size("rep") * lax.axis_size("shard")
    rows = stripe * units
    rep = lax.axis_index("rep")
    side = lax.axis_index("shard")
    quarter = rep % QUARTERS
    info = jnp.stack([side, quarter, quarter ^ 2, quarter ^ 1, quarter ^ 3]).astype(jnp.int32)

    pick, place = row_orders(assignment, stripe, groups)

    def send_rows(value):
        return dot_nn(pick, value.reshape(rows, width)).astype(BF16)

    def work_rows(value):
        return dot_nn(place, value).astype(BF16)

    token_rows = exchange(send_rows(tokens))

    lower_own = jnp.concatenate([mixer_down, merge_down, expand_down, reduce_down], axis=1)
    lower_sent = lax.dynamic_slice_in_dim(lower_own, quarter * RANK, RANK, 0)
    mixer_sent = aligned_columns(send_quarter(mixer_weight, mixer_up, quarter))
    mixer_own = (aligned_columns(mixer_weight), aligned_columns(mixer_up))
    lower_in = across(lower_sent)
    mixer_in = across(mixer_sent)
    merge_in = across(after(send_quarter(merge_weight, merge_up, quarter), mixer_in))
    expand_in = across(after(send_quarter(expand_weight, expand_up, quarter), merge_in))
    reduce_in = across(after(send_quarter(reduce_weight, reduce_up, quarter), expand_in))
    lowers = spread_quarter(lower_in)
    mixer_p = (*mixer_own, lower_own, *spread_quarter(mixer_in), *lowers)
    merge_p = (merge_weight, merge_up, lower_own, *spread_quarter(merge_in), *lowers)
    expand_p = (expand_weight, expand_up, lower_own, *spread_quarter(expand_in), *lowers)
    reduce_p = (reduce_weight, reduce_up, lower_own, *spread_quarter(reduce_in), *lowers)

    finish = jnp.cumsum(lengths[0])
    begin = finish - lengths[0]
    blocks = jnp.arange(rows // SPAN, dtype=jnp.int32)
    member = (blocks[:, None] >= begin[None, :]) & (blocks[:, None] < finish[None, :])
    first = jnp.sum(jnp.where(member, begin[None, :], 0), axis=1).astype(jnp.int32)
    owner = jnp.sum(jnp.where(member, adapter_index[None, :], 0), axis=1)
    restart = (first == blocks).astype(jnp.int32)
    position = jnp.arange(rows, dtype=jnp.int32) - jnp.repeat(first * SPAN, SPAN)
    mask = (
        jnp.repeat(owner, SPAN)[:, None] == jnp.arange(RANKS, dtype=jnp.int32)[None, :] // RANK
    ).astype(BF16)
    cosine, sines = rotation_tables(position)
    params = ssm_params(filter_taps, filter_bias, step_bias, decay_rate, skip_gain, state_gain)

    x = work_rows(token_rows)
    grad_rows = exchange(after(send_rows(cotangent), token_rows))
    united, hidden, mixer_mid = mixer_forward(info, x, mask, first_gain, mixer_p)
    attended, logs, turned, kv_low = attend_forward(united, cosine, sines, first)
    joined, scan, starts = mamba_forward(united, attended, restart, params)
    mixed, middle, second, lit, up, mids = block_forward(
        info, joined, x, mask, second_gain, merge_p, expand_p, reduce_p
    )

    def leave_rows(value):
        return exchange(lax.dot_general(
            place, value, (((0,), (0,)), ((), ())), preferred_element_type=F32
        ).astype(BF16))

    def input_rows(value, kind):
        return (
            lax.dot_general(pick, value, (((0,), (0,)), ((), ())), preferred_element_type=F32)
            .astype(kind)
            .reshape(stripe, units, width)
        )

    mixed_rows = leave_rows(mixed)

    grad_top = work_rows(grad_rows)
    dmamba, dattended, dmiddle, block_grads = block_backward(
        info, grad_top, joined, middle, second, lit, up, mids, mask, second_gain,
        merge_p, expand_p, reduce_p,
    )
    block_final = reduce_factors(block_grads)
    dquery, dkv = attend_backward(turned, kv_low, dattended, logs, cosine, sines, first)
    dunited = mamba_backward(united, scan, starts, dmamba, dquery, dkv, restart, params)
    work_grad, mixer_grads = mixer_backward(
        info, dunited, hidden, x, dmiddle, mixer_mid, mask, first_gain, mixer_p
    )
    token_grads = leave_rows(work_grad)
    mixer_final = reduce_factors(mixer_grads)
    return (
        input_rows(mixed_rows, BF16),
        input_rows(token_grads, F32),
        mixer_final[:, :D],
        given_columns(mixer_final[:, D : D + UNITED]),
        block_final[:, MERGE_L],
        block_final[:, MERGE_U],
        block_final[:, EXPAND_L],
        block_final[:, EXPAND_U],
        block_final[:, REDUCE_L],
        block_final[:, REDUCE_U],
    )


def solution(mesh):
    split = ("rep", "shard")
    sharded = P("shard", None)
    placed = (
        P(split, None, None),
        P(split, None, None),
        P(split, None),
        P(split),
        P(),
        P(),
        sharded,
        sharded,
        sharded,
        P(),
        P(),
        P(),
        P(),
        P(),
        P(),
        sharded,
        sharded,
        sharded,
        P(),
        sharded,
        sharded,
        sharded,
        sharded,
        sharded,
        sharded,
    )
    return jax.shard_map(
        on_device,
        mesh=mesh,
        in_specs=placed,
        out_specs=(P(split, None, None), P(split, None, None)) + (sharded,) * 8,
        check_vma=False,
    )
```

```python
import functools

import jax
import jax.numpy as jnp
from jax import lax
from jax.experimental import pallas as pl
from jax.experimental.pallas import tpu as pltpu
from jax.sharding import PartitionSpec as P

SSM_HEADS = 24
STATE = 128
SPAN = 128
DSSM = 1536
XBC = 1792
CONV = 4
EPS = 1e-05
NEG = -1e30
HIGH = lax.Precision.HIGHEST
F32 = jnp.float32
BF16 = jnp.bfloat16
PAIRS = DSSM // 128
HALO = 8
GATE_C = slice(0, 1536)
QUERY_C = slice(1536, 2048)
KV_C = slice(2048, 2304)
CONV_C = slice(2304, 4096)
STEP_C = slice(4096, 4224)
UNITED = 4224
GIVEN = 4120
TAIL_AT = DSSM + XBC
STEP_W = 24


def dot_nn(a, b):
    return lax.dot_general(a, b, (((1,), (0,)), ((), ())), preferred_element_type=F32)


def dot_nt(a, b):
    return lax.dot_general(a, b, (((1,), (1,)), ((), ())), preferred_element_type=F32)


def dot_exact(a, b):
    return lax.dot_general(
        a, b, (((1,), (0,)), ((), ())), precision=HIGH, preferred_element_type=F32
    )


def split_two(value):
    high = value.astype(BF16)
    return high, (value - high.astype(F32)).astype(BF16)


def spread(value, wide):
    high, rest = split_two(value)
    return dot_nn(jnp.concatenate([high, rest], axis=1), wide)


def gather_heads(value, wide):
    high, rest = split_two(value)
    narrow = wide[:SPAN]
    return dot_nt(high, narrow) + dot_nt(rest, narrow)


def softplus(value):
    return jnp.maximum(value, 0.0) + jnp.log1p(jnp.exp(-jnp.abs(value)))


def sigmoid(value):
    return 0.5 * jnp.tanh(0.5 * value) + 0.5


def iota2(dim):
    return lax.broadcasted_iota(jnp.int32, (SPAN, SPAN), dim)


def strip(number):
    return slice(number * 128, (number + 1) * 128)


def filtered(ext, taps_ref, bias_ref, cols):
    total = bias_ref[0:1, cols]
    for lag in range(CONV):
        total = total + taps_ref[lag : lag + 1, cols] * ext[HALO - lag : HALO - lag + SPAN, cols]
    return total


def mamba_forward_kernel(
    restart_ref,
    united_ref,
    attended_ref,
    taps_ref,
    bias_ref,
    step_bias_ref,
    decay_ref,
    skip_ref,
    gain_ref,
    wide_ref,
    out_ref,
    scan_ref,
    start_ref,
    ext,
    state,
    delta_w,
    grow_w,
    tail_w,
    gated_s,
):
    chunk = pl.program_id(0)
    gate_ref = united_ref.at[:, GATE_C]
    conv_ref = united_ref.at[:, CONV_C]
    step_ref = united_ref.at[:, STEP_C]
    out_ref[:, DSSM:] = attended_ref[...]

    @pl.when(restart_ref[chunk] == 1)
    def _():
        state[...] = jnp.zeros_like(state)
        ext[0:HALO, :] = jnp.zeros((HALO, XBC), F32)

    ext[HALO:, :] = conv_ref[...]
    start_ref[0] = state[...]

    step = step_ref[...] + step_bias_ref[0:1, :]
    delta = softplus(step)
    slopes = -delta * decay_ref[0:1, :]
    lower = iota2(0) >= iota2(1)
    running = dot_exact(lower.astype(F32), slopes)
    running_t = running.T
    delta_w[...] = spread(delta, wide_ref[...])
    grow_w[...] = spread(jnp.exp(running), wide_ref[...])
    tail_w[...] = spread(jnp.exp(running[SPAN - 1 :] - running), wide_ref[...])

    def convolved(cols):
        summed = filtered(ext, taps_ref, bias_ref, cols)
        return summed * sigmoid(summed)

    vec_b = convolved(slice(DSSM, DSSM + STATE))
    vec_c = convolved(slice(DSSM + STATE, XBC))
    inner = lax.dot_general(
        vec_c, vec_b, (((1,), (1,)), ((), ())), precision=HIGH, preferred_element_type=F32
    )
    low_c = vec_c.astype(BF16)
    low_bt = vec_b.T.astype(BF16)
    left = iota2(1) < 64
    squares = jnp.zeros((SPAN, SPAN), F32)
    for pair in range(PAIRS):
        cols = strip(pair)
        xs = convolved(cols)
        xd = xs * delta_w[:, cols]
        weights = []
        for head in (2 * pair, 2 * pair + 1):
            gap = running[:, head : head + 1] - running_t[head : head + 1, :]
            decays = jnp.exp(jnp.where(lower, gap, NEG))
            weights.append((inner * decays).astype(BF16))
        stacked = jnp.concatenate(
            [jnp.where(left, xd, 0.0).astype(BF16), jnp.where(left, 0.0, xd).astype(BF16)], axis=0
        )
        local = dot_nn(jnp.concatenate(weights, axis=1), stacked)
        before = state[:, cols]
        scan = local + grow_w[:, cols] * dot_nn(low_c, before.astype(BF16))
        scan_ref[:, cols] = scan
        state[:, cols] = grow_w[SPAN - 1 : SPAN, cols] * before + dot_nn(
            low_bt, (tail_w[:, cols] * xd).astype(BF16)
        )
        gate = gate_ref[:, cols]
        gated = (scan + skip_ref[0:1, cols] * xs) * (gate * sigmoid(gate))
        gated_s[:, cols] = gated
        squares = squares + gated * gated
    scale = lax.rsqrt(jnp.sum(squares, axis=1, keepdims=True) * (1.0 / DSSM) + EPS)
    for pair in range(PAIRS):
        cols = strip(pair)
        out_ref[:, cols] = (gated_s[:, cols] * scale * gain_ref[0:1, cols]).astype(BF16)
    ext[0:HALO, :] = ext[SPAN : SPAN + HALO, :]


def mamba_backward_kernel(
    restart_ref,
    united_ref,
    above_ref,
    scan_ref,
    start_ref,
    grad_ref,
    dquery_ref,
    dkv_ref,
    taps_ref,
    bias_ref,
    step_bias_ref,
    decay_ref,
    skip_ref,
    gain_ref,
    wide_ref,
    dunited_ref,
    ext,
    back,
    dstate,
    delta_w,
    grow_w,
    tail_w,
    xs_s,
    dscan_s,
    sum_s,
    cross_s,
    gain_s,
):
    gate_ref = united_ref.at[:, GATE_C]
    conv_ref = united_ref.at[:, CONV_C]
    step_ref = united_ref.at[:, STEP_C]
    before_ref = above_ref.at[:, CONV_C]
    dgate_ref = dunited_ref.at[:, :DSSM]
    dconv_ref = dunited_ref.at[:, DSSM:TAIL_AT]
    chunks = pl.num_programs(0)
    chunk = chunks - 1 - pl.program_id(0)
    following = jnp.minimum(chunk + 1, chunks - 1)

    @pl.when((chunk == chunks - 1) | (restart_ref[following] == 1))
    def _():
        dstate[...] = jnp.zeros_like(dstate)
        back[SPAN:, :] = jnp.zeros((HALO, XBC), F32)

    fresh = restart_ref[chunk] == 1
    ext[0:HALO, :] = jnp.where(fresh, 0.0, before_ref[...])
    ext[HALO:, :] = conv_ref[...]

    step = step_ref[...] + step_bias_ref[0:1, :]
    delta = softplus(step)
    slopes = -delta * decay_ref[0:1, :]
    lower = iota2(0) >= iota2(1)
    upper = iota2(0) <= iota2(1)
    running = dot_exact(lower.astype(F32), slopes)
    running_t = running.T
    delta_w[...] = spread(delta, wide_ref[...])
    grow_w[...] = spread(jnp.exp(running), wide_ref[...])
    tail_w[...] = spread(jnp.exp(running[SPAN - 1 :] - running), wide_ref[...])

    def convolved(cols):
        summed = filtered(ext, taps_ref, bias_ref, cols)
        ratio = sigmoid(summed)
        return summed * ratio, ratio * (1.0 + summed * (1.0 - ratio))

    vec_b, slope_b = convolved(slice(DSSM, DSSM + STATE))
    vec_c, slope_c = convolved(slice(DSSM + STATE, XBC))
    inner_t = lax.dot_general(
        vec_b, vec_c, (((1,), (1,)), ((), ())), precision=HIGH, preferred_element_type=F32
    )
    low_b = vec_b.astype(BF16)
    low_c = vec_c.astype(BF16)
    low_ct = vec_c.T.astype(BF16)
    left = iota2(1) < 64

    squares = jnp.zeros((SPAN, SPAN), F32)
    mixed = jnp.zeros((SPAN, SPAN), F32)
    for pair in range(PAIRS):
        cols = strip(pair)
        xs, slope = convolved(cols)
        xs_s[:, cols] = xs
        back[0:SPAN, cols] = slope
        gate = gate_ref[:, cols]
        ratio = sigmoid(gate)
        ssm = scan_ref[:, cols] + skip_ref[0:1, cols] * xs
        gated = ssm * (gate * ratio)
        dmamba = grad_ref[:, cols] * gain_ref[0:1, cols]
        squares = squares + gated * gated
        mixed = mixed + gated * dmamba
    scale = lax.rsqrt(jnp.sum(squares, axis=1, keepdims=True) * (1.0 / DSSM) + EPS)
    pull = scale * scale * scale * (jnp.sum(mixed, axis=1, keepdims=True) * (1.0 / DSSM))

    dinner_t = jnp.zeros((SPAN, SPAN), F32)
    dvec_b = jnp.zeros((SPAN, STATE), F32)
    dvec_c = jnp.zeros((SPAN, STATE), F32)
    for pair in range(PAIRS):
        cols = strip(pair)
        xs = xs_s[:, cols]
        gate = gate_ref[:, cols]
        ratio = sigmoid(gate)
        lit = gate * ratio
        scan = scan_ref[:, cols]
        ssm = scan + skip_ref[0:1, cols] * xs
        gated = ssm * lit
        dgated = scale * (grad_ref[:, cols] * gain_ref[0:1, cols]) - pull * gated
        dgate_ref[:, cols] = (dgated * ssm * (ratio * (1.0 + gate * (1.0 - ratio)))).astype(BF16)
        dscan = dgated * lit
        low_dy = dscan.astype(BF16)
        delta_c = delta_w[:, cols]
        xd = xs * delta_c
        low_xd = xd.astype(BF16)
        xd_both = jnp.concatenate(
            [jnp.where(left, xd, 0.0).astype(BF16), jnp.where(left, 0.0, xd).astype(BF16)], axis=0
        )
        dy_both = jnp.concatenate(
            [jnp.where(left, dscan, 0.0).astype(BF16), jnp.where(left, 0.0, dscan).astype(BF16)],
            axis=0,
        )
        dweights = dot_nt(xd_both, low_dy)
        weights = []
        for place, head in enumerate((2 * pair, 2 * pair + 1)):
            gap = running_t[head : head + 1, :] - running[:, head : head + 1]
            decays = jnp.exp(jnp.where(upper, gap, NEG))
            weights.append((inner_t * decays).astype(BF16))
            dinner_t = dinner_t + dweights[place * SPAN : (place + 1) * SPAN] * decays
        dxd_local = dot_nn(jnp.concatenate(weights, axis=1), dy_both)
        after = dstate[:, cols]
        low_after = after.astype(BF16)
        start = start_ref[0, :, cols]
        tail_c = tail_w[:, cols]
        grow_c = grow_w[:, cols]
        grow_last = grow_w[SPAN - 1 : SPAN, cols]
        dxd_state = tail_c * dot_nn(low_b, low_after)
        dxd = dxd_local + dxd_state
        dvec_b = dvec_b + dot_nt((tail_c * xd).astype(BF16), low_after)
        low_edy = (grow_c * dscan).astype(BF16)
        dvec_c = dvec_c + dot_nt(low_edy, start.astype(BF16))
        dstate[:, cols] = grow_last * after + dot_nn(low_ct, low_edy)
        wide_xd = low_xd.astype(F32)
        sum_s[:, cols] = low_dy.astype(F32) * scan - wide_xd * dxd
        cross_s[:, cols] = xs * dxd
        gain_s[0:8, cols] = jnp.broadcast_to(
            grow_last * jnp.sum(after * start, axis=0, keepdims=True)
            + jnp.sum(wide_xd * dxd_state, axis=0, keepdims=True),
            (8, 128),
        )
        dxs = skip_ref[0:1, cols] * dscan + delta_c * dxd
        back[0:SPAN, cols] = dxs * back[0:SPAN, cols]
    dvec_b = dvec_b + dot_nn(dinner_t.astype(BF16), low_c)
    dvec_c = dvec_c + dot_nn(dinner_t.T.astype(BF16), low_b)
    back[0:SPAN, DSSM : DSSM + STATE] = dvec_b * slope_b
    back[0:SPAN, DSSM + STATE :] = dvec_c * slope_c

    last = (iota2(0) == SPAN - 1).astype(F32)
    drunning = gather_heads(sum_s[...], wide_ref[...]) + last * gather_heads(
        gain_s[...], wide_ref[...]
    )[0:1, :]
    dslopes = dot_exact(upper.astype(F32), drunning)
    ddelta = gather_heads(cross_s[...], wide_ref[...]) - decay_ref[0:1, :] * dslopes
    dstep = ddelta * sigmoid(step)
    attention = jnp.concatenate(
        [dquery_ref[...].astype(F32), dkv_ref[...].astype(F32), jnp.zeros((SPAN, SPAN), F32)], axis=1
    )
    attention = pltpu.roll(attention, STEP_W, 1)
    dunited_ref[:, TAIL_AT : TAIL_AT + SPAN] = (attention[:, :SPAN] + dstep).astype(BF16)
    dunited_ref[:, TAIL_AT + SPAN :] = attention[:, SPAN:].astype(BF16)

    for number in range(XBC // 128):
        cols = strip(number)
        total = taps_ref[0:1, cols] * back[0:SPAN, cols]
        for lag in range(1, CONV):
            total = total + taps_ref[lag : lag + 1, cols] * back[lag : lag + SPAN, cols]
        dconv_ref[:, cols] = total.astype(BF16)
    back[SPAN:, :] = back[0:HALO, :]


def spread_matrix():
    rows = jnp.arange(2 * SPAN, dtype=jnp.int32)[:, None] % SPAN
    cols = jnp.arange(DSSM, dtype=jnp.int32)[None, :] // 64
    return (rows == cols).astype(BF16)


def pad_row(value, width):
    return jnp.pad(value, (0, width - value.shape[0]))[None, :]


def fixed(shape):
    return pl.BlockSpec(shape, lambda *_: (0,) * len(shape))


def ssm_params(filter_taps, filter_bias, step_bias, decay_rate, skip_gain, state_gain):
    return (
        filter_taps,
        filter_bias[None, :],
        pad_row(step_bias, SPAN),
        pad_row(decay_rate, SPAN),
        jnp.repeat(skip_gain, 64)[None, :],
        state_gain[None, :],
        spread_matrix(),
    )


PARAM_SPECS = [
    fixed((CONV, XBC)),
    fixed((1, XBC)),
    fixed((1, SPAN)),
    fixed((1, SPAN)),
    fixed((1, DSSM)),
    fixed((1, DSSM)),
    fixed((2 * SPAN, DSSM)),
]


def mamba_forward(united, attended, restart, params):
    rows = united.shape[0]
    chunks = rows // SPAN

    def at(width):
        return pl.BlockSpec((SPAN, width), lambda i, *_: (i, 0))

    wide = pltpu.VMEM((SPAN, DSSM), F32)
    return pl.pallas_call(
        mamba_forward_kernel,
        grid_spec=pltpu.PrefetchScalarGridSpec(
            num_scalar_prefetch=1,
            grid=(chunks,),
            in_specs=[at(UNITED), at(attended.shape[1])] + PARAM_SPECS,
            out_specs=[
                at(DSSM + attended.shape[1]),
                at(DSSM),
                pl.BlockSpec((1, STATE, DSSM), lambda i, *_: (i, 0, 0)),
            ],
            scratch_shapes=[pltpu.VMEM((SPAN + HALO, XBC), F32)] + [wide] * 5,
        ),
        out_shape=[
            jax.ShapeDtypeStruct((rows, DSSM + attended.shape[1]), BF16),
            jax.ShapeDtypeStruct((rows, DSSM), F32),
            jax.ShapeDtypeStruct((chunks, STATE, DSSM), F32),
        ],
        compiler_params=pltpu.CompilerParams(
            vmem_limit_bytes=48 << 20, dimension_semantics=("arbitrary",)
        ),
        cost_estimate=pl.CostEstimate(
            flops=20 * 10**9, bytes_accessed=50 * 10**6, transcendentals=0
        ),
        name="mamba_forward",
    )(restart, united, attended, *params)


def mamba_backward(united, scan, starts, grad, dquery, dkv, restart, params):
    rows = united.shape[0]
    chunks = rows // SPAN

    def at(width):
        return pl.BlockSpec((SPAN, width), lambda i, *_: (chunks - 1 - i, 0))

    wide = pltpu.VMEM((SPAN, DSSM), F32)
    tall = pltpu.VMEM((SPAN + HALO, XBC), F32)
    return pl.pallas_call(
        mamba_backward_kernel,
        grid_spec=pltpu.PrefetchScalarGridSpec(
            num_scalar_prefetch=1,
            grid=(chunks,),
            in_specs=[
                at(UNITED),
                pl.BlockSpec(
                    (HALO, UNITED),
                    lambda i, *_: (jnp.maximum((chunks - 1 - i) * (SPAN // HALO) - 1, 0), 0),
                ),
                at(DSSM),
                pl.BlockSpec((1, STATE, DSSM), lambda i, *_: (chunks - 1 - i, 0, 0)),
                at(DSSM),
                at(dquery.shape[1]),
                at(dkv.shape[1]),
            ]
            + PARAM_SPECS,
            out_specs=[at(UNITED)],
            scratch_shapes=[tall, tall] + [wide] * 8 + [pltpu.VMEM((8, DSSM), F32)],
        ),
        out_shape=[jax.ShapeDtypeStruct((rows, UNITED), BF16)],
        compiler_params=pltpu.CompilerParams(
            vmem_limit_bytes=48 << 20, dimension_semantics=("arbitrary",)
        ),
        cost_estimate=pl.CostEstimate(
            flops=45 * 10**9, bytes_accessed=60 * 10**6, transcendentals=0
        ),
        name="mamba_backward",
    )(restart, united, united, scan, starts, grad, dquery, dkv, *params)[0]


ATT_HEADS = 8
KV_HEADS = 2
HEAD_DIM = 64
MOST_P = 4
QUERY_W = ATT_HEADS * HEAD_DIM
KEY_W = KV_HEADS * HEAD_DIM
ROPE_BASE = 100000000000.0


def lanes_of(shape):
    return lax.broadcasted_iota(jnp.int32, shape, 1)


def turn(value, cosine, sines):
    early = (lanes_of(value.shape) // 32) % 2 == 0
    other = jnp.where(early, pltpu.roll(value, 96, 1), pltpu.roll(value, 32, 1))
    return value * cosine + other * sines


def doubled(value, head):
    left = lanes_of(value.shape) < 64
    moved = pltpu.roll(value, 64, 1)
    return jnp.where(left, value, moved) if head == 0 else jnp.where(left, moved, value)


def parted(value):
    left = lanes_of(value.shape) < 64
    return jnp.concatenate([jnp.where(left, value, 0.0), jnp.where(left, 0.0, value)], axis=0)


def joined_heads(value):
    return jnp.concatenate([value[:, :128], value[:, 128:]], axis=0).T


def causal_tail(scores, blocks):
    keys = lax.broadcasted_iota(jnp.int32, (SPAN, 2 * SPAN), 0)
    asks = lax.broadcasted_iota(jnp.int32, (SPAN, 2 * SPAN), 1) % SPAN
    tail = jnp.where(keys <= asks, scores[(blocks - 1) * SPAN :], NEG)
    if blocks == 1:
        return tail
    return jnp.concatenate([scores[: (blocks - 1) * SPAN], tail], axis=0)


def attend_forward_kernel(
    first_ref, query_ref, kv_ref, cos_ref, sin_ref, out_ref, log_ref, turned_ref, kv_low_ref, keys_s, vals_s
):
    block = pl.program_id(0)
    rows = kv_ref.shape[0]

    @pl.when(block == 0)
    def _():
        keys = turn(kv_ref[:, :KEY_W], cos_ref[...], sin_ref[...]).astype(BF16).astype(F32)
        vals = kv_ref[:, KEY_W:].astype(BF16)
        kv_low_ref[:, :KEY_W] = keys.astype(BF16)
        kv_low_ref[:, KEY_W:] = vals
        for head in range(KV_HEADS):
            keys_s[head] = doubled(keys, head).astype(BF16)
        for number in range(rows // SPAN):
            span = slice(number * SPAN, (number + 1) * SPAN)
            vals_s[:, span] = kv_ref[span, KEY_W:].T.astype(BF16)

    here = pl.ds(pl.multiple_of(block * SPAN, SPAN), SPAN)
    cosine = cos_ref[here, :]
    sines = sin_ref[here, :]
    first = first_ref[block]

    def body(blocks):
        window = pl.ds(pl.multiple_of(first * SPAN, SPAN), blocks * SPAN)
        for pair in range(ATT_HEADS // 2):
            cols = strip(pair)
            group = pair // 2
            turned = turn(query_ref[:, cols], cosine, sines).astype(BF16)
            scaled = turned.astype(F32) * (HEAD_DIM**-0.5)
            turned_ref[:, cols] = scaled.astype(BF16)
            scores = dot_nt(keys_s[group, window, :], parted(scaled).astype(BF16))
            scores = causal_tail(scores, blocks)
            peak = jnp.max(scores, axis=0, keepdims=True)
            raised = jnp.exp(scores - peak)
            total = jnp.sum(raised, axis=0, keepdims=True)
            probability = (raised * (1.0 / total)).astype(BF16)
            vals_t = vals_s[group * HEAD_DIM : (group + 1) * HEAD_DIM, window]
            out_ref[:, cols] = joined_heads(dot_nn(vals_t, probability)).astype(BF16)
            logs = peak + jnp.log(total)
            log_ref[0, 2 * pair : 2 * pair + 1, :] = logs[:, :SPAN]
            log_ref[0, 2 * pair + 1 : 2 * pair + 2, :] = logs[:, SPAN:]

    for blocks in range(1, MOST_P + 1):
        pl.when(block - first == blocks - 1)(functools.partial(body, blocks))


def attend_backward_kernel(
    first_ref,
    turned_ref,
    kv_low_ref,
    grad_ref,
    log_ref,
    cos_ref,
    sin_ref,
    dquery_ref,
    dkv_ref,
    keys_s,
    vals_s,
    keys_t,
    dkeys,
    dvals,
):
    block = pl.program_id(0)
    rows = kv_low_ref.shape[0]

    @pl.when(block == 0)
    def _():
        keys = kv_low_ref[:, :KEY_W].astype(F32)
        vals = kv_low_ref[:, KEY_W:].astype(F32)
        for head in range(KV_HEADS):
            keys_s[head] = doubled(keys, head).astype(BF16)
            vals_s[head] = doubled(vals, head).astype(BF16)
        for number in range(rows // SPAN):
            span = slice(number * SPAN, (number + 1) * SPAN)
            keys_t[:, span] = kv_low_ref[span, :KEY_W].astype(F32).T.astype(BF16)
        dkeys[...] = jnp.zeros_like(dkeys)
        dvals[...] = jnp.zeros_like(dvals)

    here = pl.ds(pl.multiple_of(block * SPAN, SPAN), SPAN)
    cosine = cos_ref[here, :]
    sines = -sin_ref[here, :]
    first = first_ref[block]

    def body(blocks):
        window = pl.ds(pl.multiple_of(first * SPAN, SPAN), blocks * SPAN)
        for pair in range(ATT_HEADS // 2):
            cols = strip(pair)
            group = pair // 2
            asks = parted(turned_ref[:, cols].astype(F32)).astype(BF16)
            grads = parted(grad_ref[:, cols].astype(F32)).astype(BF16)
            scores = causal_tail(dot_nt(keys_s[group, window, :], asks), blocks)
            logs = jnp.concatenate(
                [log_ref[0, 2 * pair : 2 * pair + 1, :], log_ref[0, 2 * pair + 1 : 2 * pair + 2, :]],
                axis=1,
            )
            probability = jnp.exp(scores - logs)
            dprob = dot_nt(vals_s[group, window, :], grads)
            inner = jnp.sum(probability * dprob, axis=0, keepdims=True)
            dscore = (probability * (dprob - inner)).astype(BF16)
            keys_g = keys_t[group * HEAD_DIM : (group + 1) * HEAD_DIM, window]
            dquery = joined_heads(dot_nn(keys_g, dscore)) * (HEAD_DIM**-0.5)
            dquery_ref[:, cols] = turn(dquery, cosine, sines).astype(BF16)
            dkeys[group, window, :] += dot_nn(dscore, asks)
            dvals[group, window, :] += dot_nn(probability.astype(BF16), grads)

    for blocks in range(1, MOST_P + 1):
        pl.when(block - first == blocks - 1)(functools.partial(body, blocks))

    @pl.when(block == pl.num_programs(0) - 1)
    def _():
        left = lanes_of((rows, KEY_W)) < 64

        def folded(total):
            sums = [total[head] + pltpu.roll(total[head], 64, 1) for head in range(KV_HEADS)]
            return jnp.where(left, sums[0], sums[1])

        dkv_ref[:, :KEY_W] = turn(folded(dkeys), cos_ref[...], -sin_ref[...]).astype(BF16)
        dkv_ref[:, KEY_W:] = folded(dvals).astype(BF16)


def rotation_tables(position):
    half = HEAD_DIM // 2
    frequency = ROPE_BASE ** (-2.0 * jnp.arange(half, dtype=F32) / HEAD_DIM)
    angles = position.astype(F32)[:, None] * frequency[None, :]
    cosine, sines = jnp.cos(angles), jnp.sin(angles)
    return (
        jnp.concatenate([cosine] * 4, axis=1),
        jnp.concatenate([-sines, sines, -sines, sines], axis=1),
    )


def attend_forward(united, cosine, sines, first):
    rows = united.shape[0]
    blocks = rows // SPAN
    at = pl.BlockSpec((SPAN, QUERY_W), lambda i, *_: (i, 0))
    query_at = pl.BlockSpec((SPAN, QUERY_W), lambda i, *_: (i, QUERY_C.start // QUERY_W))
    kv_at = pl.BlockSpec((rows, 2 * KEY_W), lambda i, *_: (0, KV_C.start // (2 * KEY_W)))
    return pl.pallas_call(
        attend_forward_kernel,
        grid_spec=pltpu.PrefetchScalarGridSpec(
            num_scalar_prefetch=1,
            grid=(blocks,),
            in_specs=[query_at, kv_at, fixed((rows, 128)), fixed((rows, 128))],
            out_specs=[
                at,
                pl.BlockSpec((1, ATT_HEADS, SPAN), lambda i, *_: (i, 0, 0)),
                at,
                fixed((rows, 2 * KEY_W)),
            ],
            scratch_shapes=[
                pltpu.VMEM((KV_HEADS, rows, 128), BF16),
                pltpu.VMEM((KEY_W, rows), BF16),
            ],
        ),
        out_shape=[
            jax.ShapeDtypeStruct((rows, QUERY_W), BF16),
            jax.ShapeDtypeStruct((blocks, ATT_HEADS, SPAN), F32),
            jax.ShapeDtypeStruct((rows, QUERY_W), BF16),
            jax.ShapeDtypeStruct((rows, 2 * KEY_W), BF16),
        ],
        compiler_params=pltpu.CompilerParams(
            vmem_limit_bytes=48 << 20, dimension_semantics=("arbitrary",)
        ),
        cost_estimate=pl.CostEstimate(
            flops=15 * 10**9, bytes_accessed=6 * 10**6, transcendentals=0
        ),
        name="attend_forward",
    )(first, united, united, cosine, sines)


def attend_backward(turned, kv_low, grad, logs, cosine, sines, first):
    rows = turned.shape[0]
    blocks = rows // SPAN
    at = pl.BlockSpec((SPAN, QUERY_W), lambda i, *_: (i, 0))
    return pl.pallas_call(
        attend_backward_kernel,
        grid_spec=pltpu.PrefetchScalarGridSpec(
            num_scalar_prefetch=1,
            grid=(blocks,),
            in_specs=[
                at,
                fixed((rows, 2 * KEY_W)),
                at,
                pl.BlockSpec((1, ATT_HEADS, SPAN), lambda i, *_: (i, 0, 0)),
                fixed((rows, 128)),
                fixed((rows, 128)),
            ],
            out_specs=[at, fixed((rows, 2 * KEY_W))],
            scratch_shapes=[
                pltpu.VMEM((KV_HEADS, rows, 128), BF16),
                pltpu.VMEM((KV_HEADS, rows, 128), BF16),
                pltpu.VMEM((KEY_W, rows), BF16),
                pltpu.VMEM((KV_HEADS, rows, 128), F32),
                pltpu.VMEM((KV_HEADS, rows, 128), F32),
            ],
        ),
        out_shape=[
            jax.ShapeDtypeStruct((rows, QUERY_W), BF16),
            jax.ShapeDtypeStruct((rows, 2 * KEY_W), BF16),
        ],
        compiler_params=pltpu.CompilerParams(
            vmem_limit_bytes=48 << 20, dimension_semantics=("arbitrary",)
        ),
        cost_estimate=pl.CostEstimate(
            flops=15 * 10**9, bytes_accessed=6 * 10**6, transcendentals=0
        ),
        name="attend_backward",
    )(first, turned, kv_low, grad, logs, cosine, sines)


RANKS = 128
ROW_BLOCK = 256
D = 1024
FF = 2048
MIX = 2048
QUARTERS = 4
ADAPT_SCALE = 0.5
COLUMN_STEP = 512
MERGE = (MIX, D, D, 4)
EXPAND = (D, 2 * FF, D + MIX, 4)
REDUCE = (FF, D, 2 * D + MIX, 2)
MIXER_CHUNKS = (slice(0, 2048), slice(2048, 4128))
OWN_ROWS = 4112
LOWER_W = 2 * D + MIX + FF
FACTORS_W = LOWER_W + UNITED


def piece_count(shape):
    return 3 + QUARTERS + shape[3]


def copy_count(shape):
    return 3 + QUARTERS + 2 * shape[3]


MIXER_PIECES = 3 + QUARTERS + QUARTERS * len(MIXER_CHUNKS)
MIXER_COPIES = 4 + 2 * QUARTERS + QUARTERS * len(MIXER_CHUNKS)


def taken(rest, *counts):
    sets = []
    for count in counts:
        sets.append(rest[:count])
        rest = rest[count:]
    return (*sets, rest)


def weight_scratch(shape):
    return [
        pltpu.VMEM((shape[0] + RANKS, shape[1]), BF16),
        pltpu.VMEM((RANKS, shape[0]), BF16),
        pltpu.SemaphoreType.DMA((copy_count(shape),)),
    ]


def mixer_scratch():
    return [
        pltpu.VMEM((UNITED, D), BF16),
        pltpu.VMEM((RANKS, UNITED), BF16),
        pltpu.VMEM((RANKS, D), BF16),
        pltpu.SemaphoreType.DMA((MIXER_COPIES,)),
    ]


def rows_at(start, count):
    return pl.ds(pl.multiple_of(start, 16), count)


def with_sems(jobs, sems):
    return [pltpu.make_async_copy(src, dst, sems.at[i]) for i, (src, dst) in enumerate(jobs)]


def factor_jobs(info_ref, own, sent, source, target):
    side = info_ref[0]
    half = RANKS // 2
    jobs = [(own.at[:, source], target.at[rows_at(side * half, half), :])]
    for number, piece in enumerate(sent):
        base = (1 - side) * half + info_ref[1 + number] * 16
        jobs.append((piece.at[:, source], target.at[rows_at(base, 16), :]))
    return jobs


def weight_copies(info_ref, shape, pieces, scratch):
    depth, _, column, parts = shape
    own_l, *sent_l = pieces[: 1 + QUARTERS]
    own_w, own_u, *sent_w = pieces[1 + QUARTERS :]
    weight, lower, sems = scratch
    side = info_ref[0]
    half, part, few = depth // 2, depth // 2 // parts, RANKS // 2 // parts
    jobs = factor_jobs(info_ref, own_l, sent_l, pl.ds(column, depth), lower)
    jobs.append((own_w, weight.at[rows_at(side * half, half), :]))
    jobs.append((own_u, weight.at[rows_at(depth + side * (RANKS // 2), RANKS // 2), :]))
    for number, sent in enumerate(sent_w):
        place = info_ref[(1 if parts == QUARTERS else 1 + QUARTERS) + number]
        start = (1 - side) * half + place * part
        base = depth + (1 - side) * (RANKS // 2) + place * few
        jobs.append((sent.at[pl.ds(0, part), :], weight.at[rows_at(start, part), :]))
        jobs.append((sent.at[pl.ds(part, few), :], weight.at[rows_at(base, few), :]))
    return with_sems(jobs, sems)


def mixer_copies(info_ref, pieces, scratch):
    own_l, *sent_l = pieces[: 1 + QUARTERS]
    own_w, own_end, *sent_w = pieces[1 + QUARTERS :]
    weight, upper, lower, sems = scratch
    side = info_ref[0]
    half, part = D // 2, D // 2 // QUARTERS

    def lanes_at(start, count):
        return pl.ds(pl.multiple_of(start, 128), count)

    jobs = factor_jobs(info_ref, own_l, sent_l, pl.ds(0, D), lower)
    jobs += factor_jobs(info_ref, own_l, sent_l, pl.ds(LOWER_W, UNITED), upper)
    mine = lanes_at(side * half, half)
    jobs.append((own_w.at[pl.ds(0, OWN_ROWS), :], weight.at[pl.ds(0, OWN_ROWS), mine]))
    jobs.append((own_end, weight.at[pl.ds(OWN_ROWS, 16), mine]))
    for number in range(QUARTERS):
        theirs = lanes_at((1 - side) * half + info_ref[1 + number] * part, part)
        for chunk, cols in enumerate(MIXER_CHUNKS):
            jobs.append((sent_w[chunk * QUARTERS + number], weight.at[cols, theirs]))
    return with_sems(jobs, sems)


def start_mixer(copies, weight):
    start_all(copies)
    end = MIXER_CHUNKS[-1].stop
    weight[end:, :] = jnp.zeros((UNITED - end, D), BF16)


def at_first(action):
    pl.when(pl.program_id(0) == 0)(action)


def start_all(copies):
    for copy in copies:
        copy.start()


def wait_all(copies):
    for copy in copies:
        copy.wait()


def halved(value):
    return (value.astype(F32) * ADAPT_SCALE).astype(BF16)


def masked(value, mask):
    return (value * mask).astype(BF16)


def norm_scale(value):
    return lax.rsqrt(jnp.sum(value * value, axis=1, keepdims=True) * (1.0 / value.shape[1]) + EPS)


def norm_back(grad, value, gain):
    scale = norm_scale(value)
    pulled = grad * gain
    inner = jnp.sum(pulled * value, axis=1, keepdims=True) * (1.0 / value.shape[1])
    return scale * pulled - value * (scale * scale * scale * inner)


def dot_tn(a, b):
    return lax.dot_general(a, b, (((0,), (0,)), ((), ())), preferred_element_type=F32)


def columns_of(width):
    return [slice(at, min(at + COLUMN_STEP, width)) for at in range(0, width, COLUMN_STEP)]


def beside_half(hidden, mid):
    return jnp.concatenate([hidden, halved(mid)], axis=1)


def mixer_forward_kernel(info_ref, x_ref, mask_ref, gain_ref, *rest):
    pieces, rest = taken(rest, MIXER_PIECES)
    united_ref, hidden_ref, mid_ref = rest[:3]
    scratch = rest[3:]
    weight, upper, lower, _ = scratch
    copies = mixer_copies(info_ref, pieces, scratch)
    at_first(lambda: start_mixer(copies, weight))
    value = x_ref[...].astype(F32)
    hidden = (value * norm_scale(value) * gain_ref[0:1, :]).astype(BF16)
    hidden_ref[...] = hidden
    at_first(lambda: wait_all(copies))
    mid = masked(dot_nt(hidden, lower[...]), mask_ref[...].astype(F32))
    mid_ref[...] = mid
    half = halved(mid)

    def projected(cols):
        return dot_nt(hidden, weight[cols, :]) + dot_nn(half, upper[:, cols])

    for start, end, shift in ((0, DSSM, 0), (DSSM, TAIL_AT, CONV_C.start - DSSM)):
        for at in range(start, end, COLUMN_STEP):
            cols = slice(at, min(at + COLUMN_STEP, end))
            united_ref[:, cols.start + shift : cols.stop + shift] = projected(cols)
    tail = projected(slice(TAIL_AT, UNITED))
    width = tail.shape[1]
    united_ref[:, DSSM : CONV_C.start] = pltpu.roll(tail, width - STEP_W, 1)[
        :, : CONV_C.start - DSSM
    ]
    steps = tail[:, :SPAN]
    united_ref[:, STEP_C] = jnp.where(lanes_of(steps.shape) < STEP_W, steps, 0.0)


MERGE_L, MERGE_U = slice(0, MIX), slice(MIX, MIX + D)
EXPAND_L, EXPAND_U = slice(MIX + D, MIX + 2 * D), slice(MIX + 2 * D, MIX + 2 * D + 2 * FF)
REDUCE_L = slice(MIX + 2 * D + 2 * FF, MIX + 2 * D + 3 * FF)
REDUCE_U = slice(MIX + 2 * D + 3 * FF, MIX + 3 * D + 3 * FF)
GRADS_W = MIX + 3 * D + 3 * FF


def add_factor_grads(total, lower_cols, upper_cols, grad_mid, hidden, mid, grad):
    gm_t = grad_mid.astype(F32).T.astype(BF16)
    mid_t = (mid.astype(F32) * ADAPT_SCALE).T.astype(BF16)
    total[:, lower_cols] += dot_nn(gm_t, hidden)
    total[:, upper_cols] += dot_nn(mid_t, grad)


def block_kernel(info_ref, joined_ref, x_ref, grad_ref, mask_ref, gain_ref, *rest):
    merge_p, expand_p, reduce_p, rest = taken(rest, *map(piece_count, (MERGE, EXPAND, REDUCE)))
    mixed_ref, dmamba_ref, dattended_ref, dmiddle_ref, grads_ref = rest[:5]
    merge_s, expand_s, reduce_s = (rest[5 + 3 * i : 8 + 3 * i] for i in range(3))
    lit_s, up_s, active_s, dexpanded_s, total = rest[14:]
    sets = [
        weight_copies(info_ref, shape, pieces, scratch)
        for shape, pieces, scratch in (
            (MERGE, merge_p, merge_s),
            (EXPAND, expand_p, expand_s),
            (REDUCE, reduce_p, reduce_s),
        )
    ]

    def begin():
        for copies in sets:
            start_all(copies)
        total[...] = jnp.zeros_like(total)

    at_first(begin)
    mask = mask_ref[...].astype(F32)
    gain = gain_ref[0:1, :]

    at_first(lambda: wait_all(sets[0]))
    weight, lower, _ = merge_s
    joined = joined_ref[...]
    merge_mid = masked(dot_nt(joined, lower[...]), mask)
    middle = x_ref[...].astype(F32) + dot_nn(beside_half(joined, merge_mid), weight[...])
    second = (middle * norm_scale(middle) * gain).astype(BF16)

    at_first(lambda: wait_all(sets[1]))
    weight, lower, _ = expand_s
    expand_mid = masked(dot_nt(second, lower[...]), mask)
    both = beside_half(second, expand_mid)
    for cols in columns_of(FF):
        lit = dot_nn(both, weight[:, cols])
        up = dot_nn(both, weight[:, FF + cols.start : FF + cols.stop])
        lit_s[:, cols] = lit
        up_s[:, cols] = up
        active_s[:, cols] = (lit * sigmoid(lit) * up).astype(BF16)

    at_first(lambda: wait_all(sets[2]))
    weight, lower, _ = reduce_s
    active = active_s[...]
    reduce_mid = masked(dot_nt(active, lower[...]), mask)
    mixed_ref[...] = (middle + dot_nn(beside_half(active, reduce_mid), weight[...])).astype(BF16)

    grad = grad_ref[...]
    grad_mid = masked(ADAPT_SCALE * dot_nt(grad, weight[FF:, :]), mask)
    for cols in columns_of(FF):
        dactive = dot_nt(grad, weight[cols, :]) + dot_nn(grad_mid, lower[:, cols])
        lit = lit_s[:, cols]
        up = up_s[:, cols]
        ratio = sigmoid(lit)
        glow = lit * ratio
        dexpanded_s[:, cols] = (dactive * up * (ratio + glow * (1.0 - ratio))).astype(BF16)
        dexpanded_s[:, FF + cols.start : FF + cols.stop] = (dactive * glow).astype(BF16)
    add_factor_grads(total, REDUCE_L, REDUCE_U, grad_mid, active, reduce_mid, grad)

    weight, lower, _ = expand_s
    dexpanded = dexpanded_s[...]
    grad_mid = masked(ADAPT_SCALE * dot_nt(dexpanded, weight[D:, :]), mask)
    dsecond = dot_nt(dexpanded, weight[:D, :]) + dot_nn(grad_mid, lower[...])
    dmiddle = grad.astype(F32) + norm_back(dsecond, middle, gain)
    dmiddle_ref[...] = dmiddle
    add_factor_grads(total, EXPAND_L, EXPAND_U, grad_mid, second, expand_mid, dexpanded)

    weight, lower, _ = merge_s
    grad = dmiddle.astype(BF16)
    grad_mid = masked(ADAPT_SCALE * dot_nt(grad, weight[MIX:, :]), mask)
    for cols in columns_of(MIX):
        djoined = dot_nt(grad, weight[cols, :]) + dot_nn(grad_mid, lower[:, cols])
        if cols.start < DSSM:
            dmamba_ref[:, cols] = djoined
        else:
            dattended_ref[...] = djoined.astype(BF16)
    add_factor_grads(total, MERGE_L, MERGE_U, grad_mid, joined, merge_mid, grad)

    @pl.when(pl.program_id(0) == pl.num_programs(0) - 1)
    def _():
        half = total.shape[1] // 2
        for place in range(2):
            grads_ref[place] = total[:, place * half : (place + 1) * half].astype(BF16)


MIXER_GRADS_W = D + UNITED + 128


def mixer_backward_kernel(
    info_ref, grad_ref, hidden_ref, x_ref, dmiddle_ref, mid_ref, mask_ref, gain_ref, *rest
):
    pieces, rest = taken(rest, MIXER_PIECES)
    out_ref, grads_ref = rest[:2]
    scratch = rest[2:6]
    total = rest[6]
    weight, upper, lower, _ = scratch
    copies = mixer_copies(info_ref, pieces, scratch)

    def begin():
        start_mixer(copies, weight)
        total[...] = jnp.zeros_like(total)

    at_first(begin)
    at_first(lambda: wait_all(copies))
    grad = grad_ref[...]
    grad_mid = masked(ADAPT_SCALE * dot_nt(grad, upper[...]), mask_ref[...].astype(F32))
    dhidden = dot_nn(grad, weight[...]) + dot_nn(grad_mid, lower[...])
    value = x_ref[...].astype(F32)
    out_ref[...] = (dmiddle_ref[...] + norm_back(dhidden, value, gain_ref[0:1, :])).astype(BF16)
    add_factor_grads(
        total,
        slice(0, D),
        slice(D, D + UNITED),
        grad_mid,
        hidden_ref[...],
        mid_ref[...],
        grad,
    )

    @pl.when(pl.program_id(0) == pl.num_programs(0) - 1)
    def _():
        half = total.shape[1] // 2
        for place in range(2):
            grads_ref[place] = total[:, place * half : (place + 1) * half].astype(BF16)


def row_call(kernel, rows, ins, fixed_ins, raw, outs, fixed_outs, scratch, info, name, flops, moved):
    def at(width):
        return pl.BlockSpec((ROW_BLOCK, width), lambda i, *_: (i, 0))

    return pl.pallas_call(
        kernel,
        grid_spec=pltpu.PrefetchScalarGridSpec(
            num_scalar_prefetch=1,
            grid=(rows // ROW_BLOCK,),
            in_specs=[at(v.shape[1]) for v in ins]
            + [fixed(v.shape) for v in fixed_ins]
            + [pl.BlockSpec(memory_space=pl.ANY)] * len(raw),
            out_specs=[at(width) for width, _ in outs] + [fixed(shape) for shape in fixed_outs],
            scratch_shapes=scratch,
        ),
        out_shape=[jax.ShapeDtypeStruct((rows, width), kind) for width, kind in outs]
        + [jax.ShapeDtypeStruct(shape, BF16) for shape in fixed_outs],
        compiler_params=pltpu.CompilerParams(
            vmem_limit_bytes=60 << 20, dimension_semantics=("arbitrary",)
        ),
        cost_estimate=pl.CostEstimate(flops=flops, bytes_accessed=moved, transcendentals=0),
        name=name,
    )(info, *ins, *fixed_ins, *raw)


def mixer_forward(info, x, mask, gain, pieces):
    rows = x.shape[0]
    return row_call(
        mixer_forward_kernel,
        rows,
        [x, mask],
        [gain[None, :]],
        pieces,
        [(UNITED, F32), (D, BF16), (RANKS, BF16)],
        [],
        mixer_scratch(),
        info,
        "mixer_forward",
        2 * rows * D * UNITED,
        2 * D * UNITED + 4 * rows * UNITED,
    )


def block(info, joined, x, grad, mask, gain, merge_p, expand_p, reduce_p):
    rows = x.shape[0]
    return row_call(
        block_kernel,
        rows,
        [joined, x, grad, mask],
        [gain[None, :]],
        [*merge_p, *expand_p, *reduce_p],
        [(D, BF16), (DSSM, F32), (MIX - DSSM, BF16), (D, F32)],
        [(2, RANKS, GRADS_W // 2)],
        weight_scratch(MERGE)
        + weight_scratch(EXPAND)
        + weight_scratch(REDUCE)
        + [
            pltpu.VMEM((ROW_BLOCK, FF), F32),
            pltpu.VMEM((ROW_BLOCK, FF), F32),
            pltpu.VMEM((ROW_BLOCK, FF), BF16),
            pltpu.VMEM((ROW_BLOCK, 2 * FF), BF16),
            pltpu.VMEM((RANKS, GRADS_W), F32),
        ],
        info,
        "block",
        5 * rows * D * (MIX + 3 * FF),
        2 * D * (MIX + 3 * FF) + 12 * rows * D,
    )


def mixer_backward(info, grad, hidden, x, dmiddle, mid, mask, gain, pieces):
    rows = x.shape[0]
    return row_call(
        mixer_backward_kernel,
        rows,
        [grad, hidden, x, dmiddle, mid, mask],
        [gain[None, :]],
        pieces,
        [(D, BF16)],
        [(2, RANKS, MIXER_GRADS_W // 2)],
        mixer_scratch() + [pltpu.VMEM((RANKS, MIXER_GRADS_W), F32)],
        info,
        "mixer_backward",
        2 * rows * D * UNITED,
        2 * D * UNITED + 8 * rows * D,
    )


SEQ_SLOTS = 3
RANK = 16


def swap_pairs(count, bit):
    return [(i, i ^ bit) for i in range(count)]


def part_of(value, parts, place, axis=0):
    size = value.shape[axis] // parts
    return lax.dynamic_slice_in_dim(value, place * size, size, axis)


def sent_rows(weight, upper, parts, place):
    return jnp.concatenate([part_of(weight, parts, place), part_of(upper, parts, place)], axis=0)


def across(value):
    return lax.ppermute(value, "shard", swap_pairs(2, 1))


def beside(value, bit):
    return lax.ppermute(value, "rep", swap_pairs(lax.axis_size("rep"), bit))


def spread_quarter(first):
    second = beside(first, 2)
    return (first, second, beside(first, 1), beside(second, 1))


def after(value, *others):
    return lax.optimization_barrier((value, *others))[0]


def core_sums(grads):
    core = lax.axis_index("rep") % 2
    kept = lax.dynamic_index_in_dim(grads, core, 0, keepdims=False)
    sent = lax.dynamic_index_in_dim(grads, 1 - core, 0, keepdims=False)
    return kept.astype(F32) + beside(sent, 1).astype(F32)


def row_sums(total, side, send):
    mine = total.shape[0] // 2
    kept = lax.dynamic_slice_in_dim(total, side * mine, mine, 0)
    sent = lax.dynamic_slice_in_dim(total, (1 - side) * mine, mine, 0).astype(BF16)
    return kept + send(sent).astype(F32)


def shard_sums(total):
    return row_sums(total, lax.axis_index("shard"), across)


def chip_bits():
    count, bits = lax.axis_size("rep") // 2, []
    while 2 ** len(bits) < count:
        bits.append(2 ** (len(bits) + 1))
    return bits


def bit_sums(total, bit):
    return row_sums(total, lax.axis_index("rep") // bit % 2, lambda value: beside(value, bit))


def ordered(mine, other, side, axis):
    return jnp.where(
        side == 0,
        jnp.concatenate([mine, other], axis=axis),
        jnp.concatenate([other, mine], axis=axis),
    )


def spread_rows(own, bits):
    rep = lax.axis_index("rep")
    for bit in reversed(bits):
        own = ordered(own, beside(own, bit), rep // bit % 2, 0)
    return ordered(own, beside(own, 1), rep % 2, 1)


def row_orders(assignment, stripe, groups):
    units = assignment.shape[0]
    per = units // groups
    total = stripe * units
    sending = jnp.arange(total, dtype=jnp.int32)
    row = sending // per % stripe
    chosen = jnp.broadcast_to(assignment.reshape(groups, 1, per), (groups, stripe, per))
    source = row * units + chosen.reshape(total)
    columns = jnp.arange(total, dtype=jnp.int32)
    pick = (source[:, None] == columns[None, :]).astype(BF16)
    working = jnp.arange(total, dtype=jnp.int32)
    piece, group, row = working // (groups * stripe), working // stripe % groups, working % stripe
    received = (group * stripe + row) * per + piece
    place = (received[:, None] == columns[None, :]).astype(BF16)
    return pick, place


def exchange(value):
    return lax.all_to_all(value, ("rep", "shard"), split_axis=0, concat_axis=0, tiled=True)


def on_device(
    tokens,
    cotangent,
    lengths,
    adapter_index,
    assignment,
    first_gain,
    mixer_weight,
    mixer_down,
    mixer_up,
    filter_taps,
    filter_bias,
    step_bias,
    decay_rate,
    skip_gain,
    state_gain,
    merge_weight,
    merge_down,
    merge_up,
    second_gain,
    expand_weight,
    expand_down,
    expand_up,
    reduce_weight,
    reduce_down,
    reduce_up,
):
    stripe, units, width = tokens.shape
    groups = lax.axis_size("rep") * lax.axis_size("shard")
    rows = stripe * units
    rep = lax.axis_index("rep")
    side = lax.axis_index("shard")
    quarter = rep % QUARTERS
    core = rep % 2
    info = jnp.stack(
        [side, quarter, quarter ^ 2, quarter ^ 1, quarter ^ 3, core, core ^ 1]
    ).astype(jnp.int32)

    pick, place = row_orders(assignment, stripe, groups)

    def send_rows(value):
        return dot_nn(pick, value.reshape(rows, width)).astype(BF16)

    def work_rows(value):
        return dot_nn(place, value).astype(BF16)

    mixer_t = mixer_weight.T
    mixer_sent = jnp.pad(part_of(mixer_t, QUARTERS, quarter, 1), ((0, 8), (0, 0)))
    mixer_sent = [mixer_sent[cols] for cols in MIXER_CHUNKS]
    mixer_in = [across(chunk) for chunk in mixer_sent]
    token_rows = exchange(send_rows(after(tokens, *mixer_sent)))
    factors = jnp.concatenate(
        [
            mixer_down,
            merge_down,
            expand_down,
            reduce_down,
            jnp.pad(mixer_up, ((0, 0), (0, UNITED - GIVEN))),
        ],
        axis=1,
    )
    factors_in = across(part_of(factors, QUARTERS, quarter))
    mixer_end = jnp.pad(mixer_t[OWN_ROWS:], ((0, OWN_ROWS + 16 - GIVEN), (0, 0)))
    grad_sent = send_rows(cotangent)
    merge_sent = sent_rows(merge_weight, merge_up, 4, quarter)
    expand_sent = sent_rows(expand_weight, expand_up, 4, quarter)
    reduce_sent = sent_rows(reduce_weight, reduce_up, 2, core)

    finish = jnp.cumsum(lengths[0])
    begin = finish - lengths[0]
    blocks = jnp.arange(rows // SPAN, dtype=jnp.int32)
    member = (blocks[:, None] >= begin[None, :]) & (blocks[:, None] < finish[None, :])
    first = jnp.sum(jnp.where(member, begin[None, :], 0), axis=1).astype(jnp.int32)
    owner = jnp.sum(jnp.where(member, adapter_index[None, :], 0), axis=1)
    restart = (first == blocks).astype(jnp.int32)
    position = jnp.arange(rows, dtype=jnp.int32) - jnp.repeat(first * SPAN, SPAN)
    mask = (
        jnp.repeat(owner, SPAN)[:, None] == jnp.arange(RANKS, dtype=jnp.int32)[None, :] // RANK
    ).astype(BF16)
    cosine, sines = rotation_tables(position)
    params = ssm_params(filter_taps, filter_bias, step_bias, decay_rate, skip_gain, state_gain)

    mixer_in[0], cosine, sines, mask, *_ = lax.optimization_barrier(
        (mixer_in[0], cosine, sines, mask, mixer_end, grad_sent, merge_sent, expand_sent, reduce_sent)
    )
    mixer_in[1] = after(mixer_in[1], mixer_in[0])
    merge_in = across(after(merge_sent, mixer_in[1]))
    lowers = (factors, *spread_quarter(factors_in))
    mixer_p = (
        *lowers,
        mixer_t,
        mixer_end,
        *spread_quarter(mixer_in[0]),
        *spread_quarter(mixer_in[1]),
    )
    expand_in = across(after(expand_sent, mixer_in[1]))
    x = work_rows(token_rows)
    grad_rows = exchange(after(grad_sent, token_rows))
    merge_in = after(merge_in, x)
    reduce_in = across(after(reduce_sent, merge_in))
    united, hidden, mixer_mid = mixer_forward(info, x, mask, first_gain, mixer_p)
    expand_in = after(expand_in, united)
    attended, logs, turned, kv_low = attend_forward(united, cosine, sines, first)
    joined, scan, starts = mamba_forward(united, attended, restart, params)

    def rest_of_quarters(first_in):
        second = beside(first_in, 2)
        return (first_in, second, beside(first_in, 1), beside(after(second, joined), 1))

    merge_p = (*lowers, merge_weight, merge_up, *rest_of_quarters(merge_in))
    expand_p = (*lowers, expand_weight, expand_up, *rest_of_quarters(expand_in))
    reduce_in = after(reduce_in, joined)
    reduce_p = (*lowers, reduce_weight, reduce_up, reduce_in, beside(reduce_in, 1))
    grad_top = work_rows(after(grad_rows, joined))
    mixed, dmamba, dattended, dmiddle, block_grads = block(
        info, joined, x, grad_top, mask, second_gain, merge_p, expand_p, reduce_p
    )

    def leaving(value):
        return lax.dot_general(
            place, value, (((0,), (0,)), ((), ())), preferred_element_type=F32
        ).astype(BF16)

    def input_rows(value, kind):
        return (
            lax.dot_general(pick, value, (((0,), (0,)), ((), ())), preferred_element_type=F32)
            .astype(kind)
            .reshape(stripe, units, width)
        )

    bits = chip_bits()
    mixed_rows = exchange(leaving(mixed))
    block_sums = core_sums(block_grads)
    dquery, dkv = attend_backward(turned, kv_low, dattended, logs, cosine, sines, first)
    dquery, block_sums = lax.optimization_barrier((dquery, block_sums))
    block_sums = shard_sums(block_sums)
    dunited = mamba_backward(united, scan, starts, dmamba, dquery, dkv, restart, params)
    dunited, block_sums, mixed_rows = lax.optimization_barrier((dunited, block_sums, mixed_rows))
    block_sums = bit_sums(block_sums, bits[0])
    work_grad, mixer_grads = mixer_backward(
        info, dunited, hidden, x, dmiddle, mixer_mid, mask, first_gain, mixer_p
    )
    work_grad, block_sums = lax.optimization_barrier((work_grad, block_sums))
    grad_leaving = leaving(work_grad)
    token_grads = exchange(grad_leaving)
    mixer_grads, block_sums, mixed_rows, _ = lax.optimization_barrier(
        (mixer_grads, block_sums, mixed_rows, grad_leaving)
    )

    def finish(_, carry):
        mixer_grads, block_sums, _ = carry
        mixer_sums = bit_sums(shard_sums(core_sums(mixer_grads)), bits[0])
        sums = jnp.concatenate([mixer_sums, block_sums], axis=1)
        for bit in bits[1:]:
            sums = bit_sums(sums, bit)
        return mixer_grads, block_sums, spread_rows(sums.astype(BF16), bits)

    width_sums = mixer_grads.shape[2] + block_sums.shape[1]
    _, _, final = lax.fori_loop(
        0,
        lax.optimization_barrier(jnp.int32(1)),
        finish,
        (mixer_grads, block_sums, jnp.zeros((RANKS // 2, 2 * width_sums), BF16)),
    )
    cut = mixer_grads.shape[2]
    final = final.reshape(RANKS // 2, 2, -1)
    mixer_final = final[:, :, :cut].reshape(RANKS // 2, -1).astype(F32)
    block_final = final[:, :, cut:].reshape(RANKS // 2, -1).astype(F32)
    mixed_out = input_rows(mixed_rows, BF16)
    return (
        mixed_out,
        input_rows(token_grads, F32),
        mixer_final[:, :D],
        mixer_final[:, D : D + GIVEN],
        block_final[:, MERGE_L],
        block_final[:, MERGE_U],
        block_final[:, EXPAND_L],
        block_final[:, EXPAND_U],
        block_final[:, REDUCE_L],
        block_final[:, REDUCE_U],
    )


def solution(mesh):
    split = ("rep", "shard")
    sharded = P("shard", None)
    placed = (
        P(split, None, None),
        P(split, None, None),
        P(split, None),
        P(split),
        P(),
        P(),
        sharded,
        sharded,
        sharded,
        P(),
        P(),
        P(),
        P(),
        P(),
        P(),
        sharded,
        sharded,
        sharded,
        P(),
        sharded,
        sharded,
        sharded,
        sharded,
        sharded,
        sharded,
    )
    return jax.shard_map(
        on_device,
        mesh=mesh,
        in_specs=placed,
        out_specs=(P(split, None, None), P(split, None, None)) + (sharded,) * 8,
        check_vma=False,
    )
```

```python
import functools

import jax
import jax.numpy as jnp
from jax import lax
from jax.experimental import pallas as pl
from jax.experimental.pallas import tpu as pltpu
from jax.sharding import PartitionSpec as P

SSM_HEADS = 24
STATE = 128
SPAN = 128
DSSM = 1536
XBC = 1792
CONV = 4
EPS = 1e-05
NEG = -1e30
HIGH = lax.Precision.HIGHEST
F32 = jnp.float32
BF16 = jnp.bfloat16
PAIRS = DSSM // 128
HALO = 8
GATE_C = slice(0, 1536)
QUERY_C = slice(1536, 2048)
KV_C = slice(2048, 2304)
CONV_C = slice(2304, 4096)
STEP_C = slice(4096, 4224)
UNITED = 4224
GIVEN = 4120
TAIL_AT = DSSM + XBC
STEP_W = 24
D = 1024
RANKS = 128
QUARTERS = 4
ADAPT_SCALE = 0.5
MIXER_GRADS_W = D + UNITED + 128


def dot_nn(a, b):
    return lax.dot_general(a, b, (((1,), (0,)), ((), ())), preferred_element_type=F32)


def dot_nt(a, b):
    return lax.dot_general(a, b, (((1,), (1,)), ((), ())), preferred_element_type=F32)


def dot_exact(a, b):
    return lax.dot_general(
        a, b, (((1,), (0,)), ((), ())), precision=HIGH, preferred_element_type=F32
    )


def split_two(value):
    high = value.astype(BF16)
    return high, (value - high.astype(F32)).astype(BF16)


def spread(value, wide):
    high, rest = split_two(value)
    return dot_nn(jnp.concatenate([high, rest], axis=1), wide)


def gather_heads(value, wide):
    high, rest = split_two(value)
    narrow = wide[:SPAN]
    return dot_nt(high, narrow) + dot_nt(rest, narrow)


def softplus(value):
    return jnp.maximum(value, 0.0) + jnp.log1p(jnp.exp(-jnp.abs(value)))


def sigmoid(value):
    return 0.5 * jnp.tanh(0.5 * value) + 0.5


def iota2(dim):
    return lax.broadcasted_iota(jnp.int32, (SPAN, SPAN), dim)


def strip(number):
    return slice(number * 128, (number + 1) * 128)


def filtered(ext, taps_ref, bias_ref, cols):
    total = bias_ref[0:1, cols]
    for lag in range(CONV):
        total = total + taps_ref[lag : lag + 1, cols] * ext[HALO - lag : HALO - lag + SPAN, cols]
    return total


def mamba_forward_kernel(
    restart_ref,
    united_ref,
    attended_ref,
    taps_ref,
    bias_ref,
    step_bias_ref,
    decay_ref,
    skip_ref,
    gain_ref,
    wide_ref,
    out_ref,
    scan_ref,
    start_ref,
    ext,
    state,
    delta_w,
    grow_w,
    tail_w,
    gated_s,
):
    chunk = pl.program_id(0)
    gate_ref = united_ref.at[:, GATE_C]
    conv_ref = united_ref.at[:, CONV_C]
    step_ref = united_ref.at[:, STEP_C]
    out_ref[:, DSSM:] = attended_ref[...]

    @pl.when(restart_ref[chunk] == 1)
    def _():
        state[...] = jnp.zeros_like(state)
        ext[0:HALO, :] = jnp.zeros((HALO, XBC), F32)

    ext[HALO:, :] = conv_ref[...]
    start_ref[0] = state[...]

    step = step_ref[...] + step_bias_ref[0:1, :]
    delta = softplus(step)
    slopes = -delta * decay_ref[0:1, :]
    lower = iota2(0) >= iota2(1)
    running = dot_exact(lower.astype(F32), slopes)
    running_t = running.T
    delta_w[...] = spread(delta, wide_ref[...])
    grow_w[...] = spread(jnp.exp(running), wide_ref[...])
    tail_w[...] = spread(jnp.exp(running[SPAN - 1 :] - running), wide_ref[...])

    def convolved(cols):
        summed = filtered(ext, taps_ref, bias_ref, cols)
        return summed * sigmoid(summed)

    vec_b = convolved(slice(DSSM, DSSM + STATE))
    vec_c = convolved(slice(DSSM + STATE, XBC))
    inner = lax.dot_general(
        vec_c, vec_b, (((1,), (1,)), ((), ())), precision=HIGH, preferred_element_type=F32
    )
    low_c = vec_c.astype(BF16)
    low_bt = vec_b.T.astype(BF16)
    left = iota2(1) < 64
    squares = jnp.zeros((SPAN, SPAN), F32)
    for pair in range(PAIRS):
        cols = strip(pair)
        xs = convolved(cols)
        xd = xs * delta_w[:, cols]
        weights = []
        for head in (2 * pair, 2 * pair + 1):
            gap = running[:, head : head + 1] - running_t[head : head + 1, :]
            decays = jnp.exp(jnp.where(lower, gap, NEG))
            weights.append((inner * decays).astype(BF16))
        stacked = jnp.concatenate(
            [jnp.where(left, xd, 0.0).astype(BF16), jnp.where(left, 0.0, xd).astype(BF16)], axis=0
        )
        local = dot_nn(jnp.concatenate(weights, axis=1), stacked)
        before = state[:, cols]
        scan = local + grow_w[:, cols] * dot_nn(low_c, before.astype(BF16))
        scan_ref[:, cols] = scan
        state[:, cols] = grow_w[SPAN - 1 : SPAN, cols] * before + dot_nn(
            low_bt, (tail_w[:, cols] * xd).astype(BF16)
        )
        gate = gate_ref[:, cols]
        gated = (scan + skip_ref[0:1, cols] * xs) * (gate * sigmoid(gate))
        gated_s[:, cols] = gated
        squares = squares + gated * gated
    scale = lax.rsqrt(jnp.sum(squares, axis=1, keepdims=True) * (1.0 / DSSM) + EPS)
    for pair in range(PAIRS):
        cols = strip(pair)
        out_ref[:, cols] = (gated_s[:, cols] * scale * gain_ref[0:1, cols]).astype(BF16)
    ext[0:HALO, :] = ext[SPAN : SPAN + HALO, :]


def mamba_backward_kernel(
    restart_ref,
    info_ref,
    united_ref,
    above_ref,
    scan_ref,
    start_ref,
    grad_ref,
    dquery_ref,
    dkv_ref,
    hidden_ref,
    mid_ref,
    mask_ref,
    taps_ref,
    bias_ref,
    step_bias_ref,
    decay_ref,
    skip_ref,
    gain_ref,
    wide_ref,
    *rest,
):
    *pieces, dunited_ref, grad_mid_ref, grads_ref = rest[: QUARTERS + 4]
    scratch = rest[QUARTERS + 4 :]
    upper, sems, total, both = scratch[-4:]
    copies = with_sems(
        factor_jobs(info_ref, pieces[0], pieces[1:], pl.ds(D, UNITED), upper), sems
    )

    def begin():
        start_all(copies)
        total[...] = jnp.zeros_like(total)

    at_first(begin)
    mamba_backward_chunk(
        restart_ref,
        united_ref,
        above_ref,
        scan_ref,
        start_ref,
        grad_ref,
        dquery_ref,
        dkv_ref,
        taps_ref,
        bias_ref,
        step_bias_ref,
        decay_ref,
        skip_ref,
        gain_ref,
        wide_ref,
        dunited_ref,
        *scratch[:-4],
    )
    at_first(lambda: wait_all(copies))
    late = pl.program_id(0) % 2 == 0

    @pl.when(late)
    def _():
        both[SPAN:, :] = dunited_ref[...]

    @pl.when(jnp.logical_not(late))
    def _():
        both[:SPAN, :] = dunited_ref[...]
        dunited = both[...]
        grad_mid = masked(ADAPT_SCALE * dot_nt(dunited, upper[...]), mask_ref[...].astype(F32))
        grad_mid_ref[...] = grad_mid
        add_factor_grads(
            total,
            slice(0, D),
            slice(D, D + UNITED),
            grad_mid,
            hidden_ref[...],
            mid_ref[...],
            dunited,
        )

    store_grads(total, grads_ref)


def mamba_backward_chunk(
    restart_ref,
    united_ref,
    above_ref,
    scan_ref,
    start_ref,
    grad_ref,
    dquery_ref,
    dkv_ref,
    taps_ref,
    bias_ref,
    step_bias_ref,
    decay_ref,
    skip_ref,
    gain_ref,
    wide_ref,
    dunited_ref,
    ext,
    back,
    dstate,
    delta_w,
    grow_w,
    tail_w,
    xs_s,
    dscan_s,
    sum_s,
    cross_s,
    gain_s,
):
    gate_ref = united_ref.at[:, GATE_C]
    conv_ref = united_ref.at[:, CONV_C]
    step_ref = united_ref.at[:, STEP_C]
    before_ref = above_ref.at[:, CONV_C]
    dgate_ref = dunited_ref.at[:, :DSSM]
    dconv_ref = dunited_ref.at[:, DSSM:TAIL_AT]
    chunks = pl.num_programs(0)
    chunk = chunks - 1 - pl.program_id(0)
    following = jnp.minimum(chunk + 1, chunks - 1)

    @pl.when((chunk == chunks - 1) | (restart_ref[following] == 1))
    def _():
        dstate[...] = jnp.zeros_like(dstate)
        back[SPAN:, :] = jnp.zeros((HALO, XBC), F32)

    fresh = restart_ref[chunk] == 1
    ext[0:HALO, :] = jnp.where(fresh, 0.0, before_ref[...])
    ext[HALO:, :] = conv_ref[...]

    step = step_ref[...] + step_bias_ref[0:1, :]
    delta = softplus(step)
    slopes = -delta * decay_ref[0:1, :]
    lower = iota2(0) >= iota2(1)
    upper = iota2(0) <= iota2(1)
    running = dot_exact(lower.astype(F32), slopes)
    running_t = running.T
    delta_w[...] = spread(delta, wide_ref[...])
    grow_w[...] = spread(jnp.exp(running), wide_ref[...])
    tail_w[...] = spread(jnp.exp(running[SPAN - 1 :] - running), wide_ref[...])

    def convolved(cols):
        summed = filtered(ext, taps_ref, bias_ref, cols)
        ratio = sigmoid(summed)
        return summed * ratio, ratio * (1.0 + summed * (1.0 - ratio))

    vec_b, slope_b = convolved(slice(DSSM, DSSM + STATE))
    vec_c, slope_c = convolved(slice(DSSM + STATE, XBC))
    inner_t = lax.dot_general(
        vec_b, vec_c, (((1,), (1,)), ((), ())), precision=HIGH, preferred_element_type=F32
    )
    low_b = vec_b.astype(BF16)
    low_c = vec_c.astype(BF16)
    low_ct = vec_c.T.astype(BF16)
    left = iota2(1) < 64

    squares = jnp.zeros((SPAN, SPAN), F32)
    mixed = jnp.zeros((SPAN, SPAN), F32)
    for pair in range(PAIRS):
        cols = strip(pair)
        xs, slope = convolved(cols)
        xs_s[:, cols] = xs
        back[0:SPAN, cols] = slope
        gate = gate_ref[:, cols]
        ratio = sigmoid(gate)
        ssm = scan_ref[:, cols] + skip_ref[0:1, cols] * xs
        gated = ssm * (gate * ratio)
        dmamba = grad_ref[:, cols] * gain_ref[0:1, cols]
        squares = squares + gated * gated
        mixed = mixed + gated * dmamba
    scale = lax.rsqrt(jnp.sum(squares, axis=1, keepdims=True) * (1.0 / DSSM) + EPS)
    pull = scale * scale * scale * (jnp.sum(mixed, axis=1, keepdims=True) * (1.0 / DSSM))

    dinner_t = jnp.zeros((SPAN, SPAN), F32)
    dvec_b = jnp.zeros((SPAN, STATE), F32)
    dvec_c = jnp.zeros((SPAN, STATE), F32)
    for pair in range(PAIRS):
        cols = strip(pair)
        xs = xs_s[:, cols]
        gate = gate_ref[:, cols]
        ratio = sigmoid(gate)
        lit = gate * ratio
        scan = scan_ref[:, cols]
        ssm = scan + skip_ref[0:1, cols] * xs
        gated = ssm * lit
        dgated = scale * (grad_ref[:, cols] * gain_ref[0:1, cols]) - pull * gated
        dgate_ref[:, cols] = (dgated * ssm * (ratio * (1.0 + gate * (1.0 - ratio)))).astype(BF16)
        dscan = dgated * lit
        low_dy = dscan.astype(BF16)
        delta_c = delta_w[:, cols]
        xd = xs * delta_c
        low_xd = xd.astype(BF16)
        xd_both = jnp.concatenate(
            [jnp.where(left, xd, 0.0).astype(BF16), jnp.where(left, 0.0, xd).astype(BF16)], axis=0
        )
        dy_both = jnp.concatenate(
            [jnp.where(left, dscan, 0.0).astype(BF16), jnp.where(left, 0.0, dscan).astype(BF16)],
            axis=0,
        )
        dweights = dot_nt(xd_both, low_dy)
        weights = []
        for place, head in enumerate((2 * pair, 2 * pair + 1)):
            gap = running_t[head : head + 1, :] - running[:, head : head + 1]
            decays = jnp.exp(jnp.where(upper, gap, NEG))
            weights.append((inner_t * decays).astype(BF16))
            dinner_t = dinner_t + dweights[place * SPAN : (place + 1) * SPAN] * decays
        dxd_local = dot_nn(jnp.concatenate(weights, axis=1), dy_both)
        after = dstate[:, cols]
        low_after = after.astype(BF16)
        start = start_ref[0, :, cols]
        tail_c = tail_w[:, cols]
        grow_c = grow_w[:, cols]
        grow_last = grow_w[SPAN - 1 : SPAN, cols]
        dxd_state = tail_c * dot_nn(low_b, low_after)
        dxd = dxd_local + dxd_state
        dvec_b = dvec_b + dot_nt((tail_c * xd).astype(BF16), low_after)
        low_edy = (grow_c * dscan).astype(BF16)
        dvec_c = dvec_c + dot_nt(low_edy, start.astype(BF16))
        dstate[:, cols] = grow_last * after + dot_nn(low_ct, low_edy)
        wide_xd = low_xd.astype(F32)
        sum_s[:, cols] = low_dy.astype(F32) * scan - wide_xd * dxd
        cross_s[:, cols] = xs * dxd
        gain_s[0:8, cols] = jnp.broadcast_to(
            grow_last * jnp.sum(after * start, axis=0, keepdims=True)
            + jnp.sum(wide_xd * dxd_state, axis=0, keepdims=True),
            (8, 128),
        )
        dxs = skip_ref[0:1, cols] * dscan + delta_c * dxd
        back[0:SPAN, cols] = dxs * back[0:SPAN, cols]
    dvec_b = dvec_b + dot_nn(dinner_t.astype(BF16), low_c)
    dvec_c = dvec_c + dot_nn(dinner_t.T.astype(BF16), low_b)
    back[0:SPAN, DSSM : DSSM + STATE] = dvec_b * slope_b
    back[0:SPAN, DSSM + STATE :] = dvec_c * slope_c

    last = (iota2(0) == SPAN - 1).astype(F32)
    drunning = gather_heads(sum_s[...], wide_ref[...]) + last * gather_heads(
        gain_s[...], wide_ref[...]
    )[0:1, :]
    dslopes = dot_exact(upper.astype(F32), drunning)
    ddelta = gather_heads(cross_s[...], wide_ref[...]) - decay_ref[0:1, :] * dslopes
    dstep = ddelta * sigmoid(step)
    attention = jnp.concatenate(
        [dquery_ref[...].astype(F32), dkv_ref[...].astype(F32), jnp.zeros((SPAN, SPAN), F32)], axis=1
    )
    attention = pltpu.roll(attention, STEP_W, 1)
    dunited_ref[:, TAIL_AT : TAIL_AT + SPAN] = (attention[:, :SPAN] + dstep).astype(BF16)
    dunited_ref[:, TAIL_AT + SPAN :] = attention[:, SPAN:].astype(BF16)

    for number in range(XBC // 128):
        cols = strip(number)
        total = taps_ref[0:1, cols] * back[0:SPAN, cols]
        for lag in range(1, CONV):
            total = total + taps_ref[lag : lag + 1, cols] * back[lag : lag + SPAN, cols]
        dconv_ref[:, cols] = total.astype(BF16)
    back[SPAN:, :] = back[0:HALO, :]


def spread_matrix():
    rows = jnp.arange(2 * SPAN, dtype=jnp.int32)[:, None] % SPAN
    cols = jnp.arange(DSSM, dtype=jnp.int32)[None, :] // 64
    return (rows == cols).astype(BF16)


def pad_row(value, width):
    return jnp.pad(value, (0, width - value.shape[0]))[None, :]


def fixed(shape):
    return pl.BlockSpec(shape, lambda *_: (0,) * len(shape))


def ssm_params(filter_taps, filter_bias, step_bias, decay_rate, skip_gain, state_gain):
    return (
        filter_taps,
        filter_bias[None, :],
        pad_row(step_bias, SPAN),
        pad_row(decay_rate, SPAN),
        jnp.repeat(skip_gain, 64)[None, :],
        state_gain[None, :],
        spread_matrix(),
    )


PARAM_SPECS = [
    fixed((CONV, XBC)),
    fixed((1, XBC)),
    fixed((1, SPAN)),
    fixed((1, SPAN)),
    fixed((1, DSSM)),
    fixed((1, DSSM)),
    fixed((2 * SPAN, DSSM)),
]


def mamba_forward(united, attended, restart, params):
    rows = united.shape[0]
    chunks = rows // SPAN

    def at(width):
        return pl.BlockSpec((SPAN, width), lambda i, *_: (i, 0))

    wide = pltpu.VMEM((SPAN, DSSM), F32)
    return pl.pallas_call(
        mamba_forward_kernel,
        grid_spec=pltpu.PrefetchScalarGridSpec(
            num_scalar_prefetch=1,
            grid=(chunks,),
            in_specs=[at(UNITED), at(attended.shape[1])] + PARAM_SPECS,
            out_specs=[
                at(DSSM + attended.shape[1]),
                at(DSSM),
                pl.BlockSpec((1, STATE, DSSM), lambda i, *_: (i, 0, 0)),
            ],
            scratch_shapes=[pltpu.VMEM((SPAN + HALO, XBC), F32)] + [wide] * 5,
        ),
        out_shape=[
            jax.ShapeDtypeStruct((rows, DSSM + attended.shape[1]), BF16),
            jax.ShapeDtypeStruct((rows, DSSM), F32),
            jax.ShapeDtypeStruct((chunks, STATE, DSSM), F32),
        ],
        compiler_params=pltpu.CompilerParams(
            vmem_limit_bytes=48 << 20, dimension_semantics=("arbitrary",)
        ),
        cost_estimate=pl.CostEstimate(
            flops=20 * 10**9, bytes_accessed=50 * 10**6, transcendentals=0
        ),
        name="mamba_forward",
    )(restart, united, attended, *params)


def mamba_backward(
    united, scan, starts, grad, dquery, dkv, hidden, mid, mask, restart, info, params, factors
):
    rows = united.shape[0]
    chunks = rows // SPAN

    def at(width):
        return pl.BlockSpec((SPAN, width), lambda i, *_: (chunks - 1 - i, 0))

    def at_two(width):
        return pl.BlockSpec((2 * SPAN, width), lambda i, *_: ((chunks - 1 - i) // 2, 0))

    wide = pltpu.VMEM((SPAN, DSSM), F32)
    tall = pltpu.VMEM((SPAN + HALO, XBC), F32)
    return pl.pallas_call(
        mamba_backward_kernel,
        grid_spec=pltpu.PrefetchScalarGridSpec(
            num_scalar_prefetch=2,
            grid=(chunks,),
            in_specs=[
                at(UNITED),
                pl.BlockSpec(
                    (HALO, UNITED),
                    lambda i, *_: (jnp.maximum((chunks - 1 - i) * (SPAN // HALO) - 1, 0), 0),
                ),
                at(DSSM),
                pl.BlockSpec((1, STATE, DSSM), lambda i, *_: (chunks - 1 - i, 0, 0)),
                at(DSSM),
                at(dquery.shape[1]),
                at(dkv.shape[1]),
                at_two(D),
                at_two(RANKS),
                at_two(RANKS),
            ]
            + PARAM_SPECS
            + [pl.BlockSpec(memory_space=pl.ANY)] * (1 + QUARTERS),
            out_specs=[at(UNITED), at_two(RANKS), fixed((2, RANKS, MIXER_GRADS_W // 2))],
            scratch_shapes=[tall, tall]
            + [wide] * 8
            + [
                pltpu.VMEM((8, DSSM), F32),
                pltpu.VMEM((RANKS, UNITED), BF16),
                pltpu.SemaphoreType.DMA((1 + QUARTERS,)),
                pltpu.VMEM((RANKS, MIXER_GRADS_W), F32),
                pltpu.VMEM((2 * SPAN, UNITED), BF16),
            ],
        ),
        out_shape=[
            jax.ShapeDtypeStruct((rows, UNITED), BF16),
            jax.ShapeDtypeStruct((rows, RANKS), BF16),
            jax.ShapeDtypeStruct((2, RANKS, MIXER_GRADS_W // 2), BF16),
        ],
        compiler_params=pltpu.CompilerParams(
            vmem_limit_bytes=56 << 20, dimension_semantics=("arbitrary",)
        ),
        cost_estimate=pl.CostEstimate(
            flops=45 * 10**9, bytes_accessed=60 * 10**6, transcendentals=0
        ),
        name="mamba_backward",
    )(
        restart, info, united, united, scan, starts, grad, dquery, dkv, hidden, mid, mask,
        *params, *factors,
    )


ATT_HEADS = 8
KV_HEADS = 2
HEAD_DIM = 64
MOST_P = 4
QUERY_W = ATT_HEADS * HEAD_DIM
KEY_W = KV_HEADS * HEAD_DIM
ROPE_BASE = 100000000000.0


def lanes_of(shape):
    return lax.broadcasted_iota(jnp.int32, shape, 1)


def turn(value, cosine, sines):
    early = (lanes_of(value.shape) // 32) % 2 == 0
    other = jnp.where(early, pltpu.roll(value, 96, 1), pltpu.roll(value, 32, 1))
    return value * cosine + other * sines


def doubled(value, head):
    left = lanes_of(value.shape) < 64
    moved = pltpu.roll(value, 64, 1)
    return jnp.where(left, value, moved) if head == 0 else jnp.where(left, moved, value)


def parted(value):
    left = lanes_of(value.shape) < 64
    return jnp.concatenate([jnp.where(left, value, 0.0), jnp.where(left, 0.0, value)], axis=0)


def joined_heads(value):
    return jnp.concatenate([value[:, :128], value[:, 128:]], axis=0).T


def causal_tail(scores, blocks):
    keys = lax.broadcasted_iota(jnp.int32, (SPAN, 2 * SPAN), 0)
    asks = lax.broadcasted_iota(jnp.int32, (SPAN, 2 * SPAN), 1) % SPAN
    tail = jnp.where(keys <= asks, scores[(blocks - 1) * SPAN :], NEG)
    if blocks == 1:
        return tail
    return jnp.concatenate([scores[: (blocks - 1) * SPAN], tail], axis=0)


def attend_forward_kernel(
    first_ref, query_ref, kv_ref, cos_ref, sin_ref, out_ref, log_ref, turned_ref, kv_low_ref, keys_s, vals_s
):
    block = pl.program_id(0)
    rows = kv_ref.shape[0]

    @pl.when(block == 0)
    def _():
        keys = turn(kv_ref[:, :KEY_W], cos_ref[...], sin_ref[...]).astype(BF16).astype(F32)
        vals = kv_ref[:, KEY_W:].astype(BF16)
        kv_low_ref[:, :KEY_W] = keys.astype(BF16)
        kv_low_ref[:, KEY_W:] = vals
        for head in range(KV_HEADS):
            keys_s[head] = doubled(keys, head).astype(BF16)
        for number in range(rows // SPAN):
            span = slice(number * SPAN, (number + 1) * SPAN)
            vals_s[:, span] = kv_ref[span, KEY_W:].T.astype(BF16)

    here = pl.ds(pl.multiple_of(block * SPAN, SPAN), SPAN)
    cosine = cos_ref[here, :]
    sines = sin_ref[here, :]
    first = first_ref[block]

    def body(blocks):
        window = pl.ds(pl.multiple_of(first * SPAN, SPAN), blocks * SPAN)
        for pair in range(ATT_HEADS // 2):
            cols = strip(pair)
            group = pair // 2
            turned = turn(query_ref[:, cols], cosine, sines).astype(BF16)
            scaled = turned.astype(F32) * (HEAD_DIM**-0.5)
            turned_ref[:, cols] = scaled.astype(BF16)
            scores = dot_nt(keys_s[group, window, :], parted(scaled).astype(BF16))
            scores = causal_tail(scores, blocks)
            peak = jnp.max(scores, axis=0, keepdims=True)
            raised = jnp.exp(scores - peak)
            total = jnp.sum(raised, axis=0, keepdims=True)
            probability = (raised * (1.0 / total)).astype(BF16)
            vals_t = vals_s[group * HEAD_DIM : (group + 1) * HEAD_DIM, window]
            out_ref[:, cols] = joined_heads(dot_nn(vals_t, probability)).astype(BF16)
            logs = peak + jnp.log(total)
            log_ref[0, 2 * pair : 2 * pair + 1, :] = logs[:, :SPAN]
            log_ref[0, 2 * pair + 1 : 2 * pair + 2, :] = logs[:, SPAN:]

    for blocks in range(1, MOST_P + 1):
        pl.when(block - first == blocks - 1)(functools.partial(body, blocks))


def attend_backward_kernel(
    first_ref,
    turned_ref,
    kv_low_ref,
    grad_ref,
    log_ref,
    cos_ref,
    sin_ref,
    dquery_ref,
    dkv_ref,
    keys_s,
    vals_s,
    keys_t,
    dkeys,
    dvals,
):
    block = pl.program_id(0)
    rows = kv_low_ref.shape[0]

    @pl.when(block == 0)
    def _():
        keys = kv_low_ref[:, :KEY_W].astype(F32)
        vals = kv_low_ref[:, KEY_W:].astype(F32)
        for head in range(KV_HEADS):
            keys_s[head] = doubled(keys, head).astype(BF16)
            vals_s[head] = doubled(vals, head).astype(BF16)
        for number in range(rows // SPAN):
            span = slice(number * SPAN, (number + 1) * SPAN)
            keys_t[:, span] = kv_low_ref[span, :KEY_W].astype(F32).T.astype(BF16)
        dkeys[...] = jnp.zeros_like(dkeys)
        dvals[...] = jnp.zeros_like(dvals)

    here = pl.ds(pl.multiple_of(block * SPAN, SPAN), SPAN)
    cosine = cos_ref[here, :]
    sines = -sin_ref[here, :]
    first = first_ref[block]

    def body(blocks):
        window = pl.ds(pl.multiple_of(first * SPAN, SPAN), blocks * SPAN)
        for pair in range(ATT_HEADS // 2):
            cols = strip(pair)
            group = pair // 2
            asks = parted(turned_ref[:, cols].astype(F32)).astype(BF16)
            grads = parted(grad_ref[:, cols].astype(F32)).astype(BF16)
            scores = causal_tail(dot_nt(keys_s[group, window, :], asks), blocks)
            logs = jnp.concatenate(
                [log_ref[0, 2 * pair : 2 * pair + 1, :], log_ref[0, 2 * pair + 1 : 2 * pair + 2, :]],
                axis=1,
            )
            probability = jnp.exp(scores - logs)
            dprob = dot_nt(vals_s[group, window, :], grads)
            inner = jnp.sum(probability * dprob, axis=0, keepdims=True)
            dscore = (probability * (dprob - inner)).astype(BF16)
            keys_g = keys_t[group * HEAD_DIM : (group + 1) * HEAD_DIM, window]
            dquery = joined_heads(dot_nn(keys_g, dscore)) * (HEAD_DIM**-0.5)
            dquery_ref[:, cols] = turn(dquery, cosine, sines).astype(BF16)
            dkeys[group, window, :] += dot_nn(dscore, asks)
            dvals[group, window, :] += dot_nn(probability.astype(BF16), grads)

    for blocks in range(1, MOST_P + 1):
        pl.when(block - first == blocks - 1)(functools.partial(body, blocks))

    @pl.when(block == pl.num_programs(0) - 1)
    def _():
        left = lanes_of((rows, KEY_W)) < 64

        def folded(total):
            sums = [total[head] + pltpu.roll(total[head], 64, 1) for head in range(KV_HEADS)]
            return jnp.where(left, sums[0], sums[1])

        dkv_ref[:, :KEY_W] = turn(folded(dkeys), cos_ref[...], -sin_ref[...]).astype(BF16)
        dkv_ref[:, KEY_W:] = folded(dvals).astype(BF16)


def rotation_tables(position):
    half = HEAD_DIM // 2
    frequency = ROPE_BASE ** (-2.0 * jnp.arange(half, dtype=F32) / HEAD_DIM)
    angles = position.astype(F32)[:, None] * frequency[None, :]
    cosine, sines = jnp.cos(angles), jnp.sin(angles)
    return (
        jnp.concatenate([cosine] * 4, axis=1),
        jnp.concatenate([-sines, sines, -sines, sines], axis=1),
    )


def attend_forward(united, cosine, sines, first):
    rows = united.shape[0]
    blocks = rows // SPAN
    at = pl.BlockSpec((SPAN, QUERY_W), lambda i, *_: (i, 0))
    query_at = pl.BlockSpec((SPAN, QUERY_W), lambda i, *_: (i, QUERY_C.start // QUERY_W))
    kv_at = pl.BlockSpec((rows, 2 * KEY_W), lambda i, *_: (0, KV_C.start // (2 * KEY_W)))
    return pl.pallas_call(
        attend_forward_kernel,
        grid_spec=pltpu.PrefetchScalarGridSpec(
            num_scalar_prefetch=1,
            grid=(blocks,),
            in_specs=[query_at, kv_at, fixed((rows, 128)), fixed((rows, 128))],
            out_specs=[
                at,
                pl.BlockSpec((1, ATT_HEADS, SPAN), lambda i, *_: (i, 0, 0)),
                at,
                fixed((rows, 2 * KEY_W)),
            ],
            scratch_shapes=[
                pltpu.VMEM((KV_HEADS, rows, 128), BF16),
                pltpu.VMEM((KEY_W, rows), BF16),
            ],
        ),
        out_shape=[
            jax.ShapeDtypeStruct((rows, QUERY_W), BF16),
            jax.ShapeDtypeStruct((blocks, ATT_HEADS, SPAN), F32),
            jax.ShapeDtypeStruct((rows, QUERY_W), BF16),
            jax.ShapeDtypeStruct((rows, 2 * KEY_W), BF16),
        ],
        compiler_params=pltpu.CompilerParams(
            vmem_limit_bytes=48 << 20, dimension_semantics=("arbitrary",)
        ),
        cost_estimate=pl.CostEstimate(
            flops=15 * 10**9, bytes_accessed=6 * 10**6, transcendentals=0
        ),
        name="attend_forward",
    )(first, united, united, cosine, sines)


def attend_backward(turned, kv_low, grad, logs, cosine, sines, first):
    rows = turned.shape[0]
    blocks = rows // SPAN
    at = pl.BlockSpec((SPAN, QUERY_W), lambda i, *_: (i, 0))
    return pl.pallas_call(
        attend_backward_kernel,
        grid_spec=pltpu.PrefetchScalarGridSpec(
            num_scalar_prefetch=1,
            grid=(blocks,),
            in_specs=[
                at,
                fixed((rows, 2 * KEY_W)),
                at,
                pl.BlockSpec((1, ATT_HEADS, SPAN), lambda i, *_: (i, 0, 0)),
                fixed((rows, 128)),
                fixed((rows, 128)),
            ],
            out_specs=[at, fixed((rows, 2 * KEY_W))],
            scratch_shapes=[
                pltpu.VMEM((KV_HEADS, rows, 128), BF16),
                pltpu.VMEM((KV_HEADS, rows, 128), BF16),
                pltpu.VMEM((KEY_W, rows), BF16),
                pltpu.VMEM((KV_HEADS, rows, 128), F32),
                pltpu.VMEM((KV_HEADS, rows, 128), F32),
            ],
        ),
        out_shape=[
            jax.ShapeDtypeStruct((rows, QUERY_W), BF16),
            jax.ShapeDtypeStruct((rows, 2 * KEY_W), BF16),
        ],
        compiler_params=pltpu.CompilerParams(
            vmem_limit_bytes=48 << 20, dimension_semantics=("arbitrary",)
        ),
        cost_estimate=pl.CostEstimate(
            flops=15 * 10**9, bytes_accessed=6 * 10**6, transcendentals=0
        ),
        name="attend_backward",
    )(first, turned, kv_low, grad, logs, cosine, sines)


ROW_BLOCK = 256
FF = 2048
MIX = 2048
COLUMN_STEP = 512
MERGE = (MIX, D, 0, 4, (slice(0, D),))
EXPAND = (D, 2 * FF, MIX, 4, (slice(0, FF), slice(FF, 2 * FF)))
REDUCE = (FF, D, D + MIX, 2, (slice(0, D),))
MIXER_CHUNKS = (slice(0, 2048), slice(2048, 4128))
OWN_ROWS = 4112
def piece_count(shape):
    return 3 + QUARTERS + shape[3] * len(shape[4])


def copy_count(shape):
    return 3 + QUARTERS + 2 * shape[3] * len(shape[4])


MIXER_PIECES = 3 + QUARTERS + QUARTERS * len(MIXER_CHUNKS)
MIXER_COPIES = 4 + 2 * QUARTERS + QUARTERS * len(MIXER_CHUNKS)


def taken(rest, *counts):
    sets = []
    for count in counts:
        sets.append(rest[:count])
        rest = rest[count:]
    return (*sets, rest)


def weight_scratch(shape):
    return [
        pltpu.VMEM((shape[0] + RANKS, shape[1]), BF16),
        pltpu.VMEM((RANKS, shape[0]), BF16),
        pltpu.SemaphoreType.DMA((copy_count(shape),)),
    ]


def mixer_scratch():
    return [
        pltpu.VMEM((UNITED, D), BF16),
        pltpu.VMEM((RANKS, UNITED), BF16),
        pltpu.VMEM((RANKS, D), BF16),
        pltpu.SemaphoreType.DMA((MIXER_COPIES,)),
    ]


def rows_at(start, count):
    return pl.ds(pl.multiple_of(start, 16), count)


def with_sems(jobs, sems):
    return [pltpu.make_async_copy(src, dst, sems.at[i]) for i, (src, dst) in enumerate(jobs)]


def factor_jobs(info_ref, own, sent, source, target):
    side = info_ref[0]
    half = RANKS // 2
    jobs = [(own.at[:, source], target.at[rows_at(side * half, half), :])]
    for number, piece in enumerate(sent):
        base = (1 - side) * half + info_ref[1 + number] * 16
        jobs.append((piece.at[:, source], target.at[rows_at(base, 16), :]))
    return jobs


def weight_copies(info_ref, shape, pieces, scratch):
    depth, _, column, parts, chunks = shape
    own_l, *sent_l = pieces[: 1 + QUARTERS]
    own_w, own_u, *sent_w = pieces[1 + QUARTERS :]
    weight, lower, sems = scratch
    side = info_ref[0]
    half, part, few = depth // 2, depth // 2 // parts, RANKS // 2 // parts
    jobs = factor_jobs(info_ref, own_l, sent_l, pl.ds(column, depth), lower)
    jobs.append((own_w, weight.at[rows_at(side * half, half), :]))
    jobs.append((own_u, weight.at[rows_at(depth + side * (RANKS // 2), RANKS // 2), :]))
    for number in range(parts):
        place = info_ref[(1 if parts == QUARTERS else 1 + QUARTERS) + number]
        start = (1 - side) * half + place * part
        base = depth + (1 - side) * (RANKS // 2) + place * few
        for chunk, cols in enumerate(chunks):
            sent = sent_w[chunk * parts + number]
            jobs.append((sent.at[pl.ds(0, part), :], weight.at[rows_at(start, part), cols]))
            jobs.append((sent.at[pl.ds(part, few), :], weight.at[rows_at(base, few), cols]))
    return with_sems(jobs, sems)


def mixer_copies(info_ref, pieces, scratch):
    own_l, *sent_l = pieces[: 1 + QUARTERS]
    own_w, own_end, *sent_w = pieces[1 + QUARTERS :]
    weight, upper, lower, sems = scratch
    side = info_ref[0]
    half, part = D // 2, D // 2 // QUARTERS

    def lanes_at(start, count):
        return pl.ds(pl.multiple_of(start, 128), count)

    jobs = factor_jobs(info_ref, own_l, sent_l, pl.ds(0, D), lower)
    jobs += factor_jobs(info_ref, own_l, sent_l, pl.ds(D, UNITED), upper)
    mine = lanes_at(side * half, half)
    jobs.append((own_w.at[pl.ds(0, OWN_ROWS), :], weight.at[pl.ds(0, OWN_ROWS), mine]))
    jobs.append((own_end, weight.at[pl.ds(OWN_ROWS, 16), mine]))
    for number in range(QUARTERS):
        theirs = lanes_at((1 - side) * half + info_ref[1 + number] * part, part)
        for chunk, cols in enumerate(MIXER_CHUNKS):
            jobs.append((sent_w[chunk * QUARTERS + number], weight.at[cols, theirs]))
    return with_sems(jobs, sems)


def start_mixer(copies, weight):
    start_all(copies)
    end = MIXER_CHUNKS[-1].stop
    weight[end:, :] = jnp.zeros((UNITED - end, D), BF16)


def at_first(action):
    pl.when(pl.program_id(0) == 0)(action)


def start_all(copies):
    for copy in copies:
        copy.start()


def wait_all(copies):
    for copy in copies:
        copy.wait()


def halved(value):
    return (value.astype(F32) * ADAPT_SCALE).astype(BF16)


def masked(value, mask):
    return (value * mask).astype(BF16)


def norm_scale(value):
    return lax.rsqrt(jnp.sum(value * value, axis=1, keepdims=True) * (1.0 / value.shape[1]) + EPS)


def norm_back(grad, value, gain):
    scale = norm_scale(value)
    pulled = grad * gain
    inner = jnp.sum(pulled * value, axis=1, keepdims=True) * (1.0 / value.shape[1])
    return scale * pulled - value * (scale * scale * scale * inner)


def dot_tn(a, b):
    return lax.dot_general(a, b, (((0,), (0,)), ((), ())), preferred_element_type=F32)


def columns_of(width):
    return [slice(at, min(at + COLUMN_STEP, width)) for at in range(0, width, COLUMN_STEP)]


def beside_half(hidden, mid):
    return jnp.concatenate([hidden, halved(mid)], axis=1)


def mixer_forward_kernel(info_ref, x_ref, mask_ref, gain_ref, *rest):
    pieces, rest = taken(rest, MIXER_PIECES)
    united_ref, hidden_ref, mid_ref = rest[:3]
    scratch = rest[3:]
    weight, upper, lower, _ = scratch
    copies = mixer_copies(info_ref, pieces, scratch)
    at_first(lambda: start_mixer(copies, weight))
    value = x_ref[...].astype(F32)
    hidden = (value * norm_scale(value) * gain_ref[0:1, :]).astype(BF16)
    hidden_ref[...] = hidden
    at_first(lambda: wait_all(copies))
    mid = masked(dot_nt(hidden, lower[...]), mask_ref[...].astype(F32))
    mid_ref[...] = mid
    half = halved(mid)

    def projected(cols):
        return dot_nt(hidden, weight[cols, :]) + dot_nn(half, upper[:, cols])

    for start, end, shift in ((0, DSSM, 0), (DSSM, TAIL_AT, CONV_C.start - DSSM)):
        for at in range(start, end, COLUMN_STEP):
            cols = slice(at, min(at + COLUMN_STEP, end))
            united_ref[:, cols.start + shift : cols.stop + shift] = projected(cols)
    tail = projected(slice(TAIL_AT, UNITED))
    width = tail.shape[1]
    united_ref[:, DSSM : CONV_C.start] = pltpu.roll(tail, width - STEP_W, 1)[
        :, : CONV_C.start - DSSM
    ]
    steps = tail[:, :SPAN]
    united_ref[:, STEP_C] = jnp.where(lanes_of(steps.shape) < STEP_W, steps, 0.0)


MERGE_L, MERGE_U = slice(0, MIX), slice(MIX, MIX + D)
EXPAND_L, EXPAND_U = slice(MIX + D, MIX + 2 * D), slice(MIX + 2 * D, MIX + 2 * D + 2 * FF)
REDUCE_L = slice(MIX + 2 * D + 2 * FF, MIX + 2 * D + 3 * FF)
REDUCE_U = slice(MIX + 2 * D + 3 * FF, MIX + 3 * D + 3 * FF)
GRADS_W = MIX + 3 * D + 3 * FF


def store_grads(total, grads_ref):
    @pl.when(pl.program_id(0) == pl.num_programs(0) - 1)
    def _():
        half = total.shape[1] // 2
        for place in range(2):
            grads_ref[place] = total[:, place * half : (place + 1) * half].astype(BF16)


def add_factor_grads(total, lower_cols, upper_cols, grad_mid, hidden, mid, grad):
    gm_t = grad_mid.astype(F32).T.astype(BF16)
    mid_t = (mid.astype(F32) * ADAPT_SCALE).T.astype(BF16)
    total[:, lower_cols] += dot_nn(gm_t, hidden)
    total[:, upper_cols] += dot_nn(mid_t, grad)


def block_kernel(info_ref, joined_ref, x_ref, grad_ref, mask_ref, gain_ref, *rest):
    merge_p, expand_p, reduce_p, rest = taken(rest, *map(piece_count, (MERGE, EXPAND, REDUCE)))
    mixed_ref, dmamba_ref, dattended_ref, dmiddle_ref, grads_ref = rest[:5]
    merge_s, expand_s, reduce_s = (rest[5 + 3 * i : 8 + 3 * i] for i in range(3))
    lit_s, up_s, active_s, dexpanded_s, total = rest[14:]
    sets = [
        weight_copies(info_ref, shape, pieces, scratch)
        for shape, pieces, scratch in (
            (MERGE, merge_p, merge_s),
            (EXPAND, expand_p, expand_s),
            (REDUCE, reduce_p, reduce_s),
        )
    ]

    def begin():
        for copies in sets:
            start_all(copies)
        total[...] = jnp.zeros_like(total)

    at_first(begin)
    mask = mask_ref[...].astype(F32)
    gain = gain_ref[0:1, :]

    at_first(lambda: wait_all(sets[0]))
    weight, lower, _ = merge_s
    joined = joined_ref[...]
    merge_mid = masked(dot_nt(joined, lower[...]), mask)
    middle = x_ref[...].astype(F32) + dot_nn(beside_half(joined, merge_mid), weight[...])
    second = (middle * norm_scale(middle) * gain).astype(BF16)

    at_first(lambda: wait_all(sets[1]))
    weight, lower, _ = expand_s
    expand_mid = masked(dot_nt(second, lower[...]), mask)
    both = beside_half(second, expand_mid)
    for cols in columns_of(FF):
        lit = dot_nn(both, weight[:, cols])
        up = dot_nn(both, weight[:, FF + cols.start : FF + cols.stop])
        lit_s[:, cols] = lit
        up_s[:, cols] = up
        active_s[:, cols] = (lit * sigmoid(lit) * up).astype(BF16)

    at_first(lambda: wait_all(sets[2]))
    weight, lower, _ = reduce_s
    active = active_s[...]
    reduce_mid = masked(dot_nt(active, lower[...]), mask)
    mixed_ref[...] = (middle + dot_nn(beside_half(active, reduce_mid), weight[...])).astype(BF16)

    grad = grad_ref[...]
    grad_mid = masked(ADAPT_SCALE * dot_nt(grad, weight[FF:, :]), mask)
    for cols in columns_of(FF):
        dactive = dot_nt(grad, weight[cols, :]) + dot_nn(grad_mid, lower[:, cols])
        lit = lit_s[:, cols]
        up = up_s[:, cols]
        ratio = sigmoid(lit)
        glow = lit * ratio
        dexpanded_s[:, cols] = (dactive * up * (ratio + glow * (1.0 - ratio))).astype(BF16)
        dexpanded_s[:, FF + cols.start : FF + cols.stop] = (dactive * glow).astype(BF16)
    add_factor_grads(total, REDUCE_L, REDUCE_U, grad_mid, active, reduce_mid, grad)

    weight, lower, _ = expand_s
    dexpanded = dexpanded_s[...]
    grad_mid = masked(ADAPT_SCALE * dot_nt(dexpanded, weight[D:, :]), mask)
    dsecond = dot_nt(dexpanded, weight[:D, :]) + dot_nn(grad_mid, lower[...])
    dmiddle = grad.astype(F32) + norm_back(dsecond, middle, gain)
    dmiddle_ref[...] = dmiddle
    add_factor_grads(total, EXPAND_L, EXPAND_U, grad_mid, second, expand_mid, dexpanded)

    weight, lower, _ = merge_s
    grad = dmiddle.astype(BF16)
    grad_mid = masked(ADAPT_SCALE * dot_nt(grad, weight[MIX:, :]), mask)
    for cols in columns_of(MIX):
        djoined = dot_nt(grad, weight[cols, :]) + dot_nn(grad_mid, lower[:, cols])
        if cols.start < DSSM:
            dmamba_ref[:, cols] = djoined
        else:
            dattended_ref[...] = djoined.astype(BF16)
    add_factor_grads(total, MERGE_L, MERGE_U, grad_mid, joined, merge_mid, grad)

    store_grads(total, grads_ref)


def mixer_backward_kernel(
    info_ref, grad_ref, grad_mid_ref, x_ref, dmiddle_ref, gain_ref, *rest
):
    pieces, rest = taken(rest, MIXER_PIECES)
    out_ref, *scratch = rest
    weight, _, lower, _ = scratch
    copies = mixer_copies(info_ref, pieces, scratch)
    at_first(lambda: start_mixer(copies, weight))
    at_first(lambda: wait_all(copies))
    dhidden = dot_nn(grad_ref[...], weight[...]) + dot_nn(grad_mid_ref[...], lower[...])
    value = x_ref[...].astype(F32)
    out_ref[...] = (dmiddle_ref[...] + norm_back(dhidden, value, gain_ref[0:1, :])).astype(BF16)


def row_call(kernel, rows, ins, fixed_ins, raw, outs, fixed_outs, scratch, info, name, flops, moved):
    def at(width):
        return pl.BlockSpec((ROW_BLOCK, width), lambda i, *_: (i, 0))

    return pl.pallas_call(
        kernel,
        grid_spec=pltpu.PrefetchScalarGridSpec(
            num_scalar_prefetch=1,
            grid=(rows // ROW_BLOCK,),
            in_specs=[at(v.shape[1]) for v in ins]
            + [fixed(v.shape) for v in fixed_ins]
            + [pl.BlockSpec(memory_space=pl.ANY)] * len(raw),
            out_specs=[at(width) for width, _ in outs] + [fixed(shape) for shape in fixed_outs],
            scratch_shapes=scratch,
        ),
        out_shape=[jax.ShapeDtypeStruct((rows, width), kind) for width, kind in outs]
        + [jax.ShapeDtypeStruct(shape, BF16) for shape in fixed_outs],
        compiler_params=pltpu.CompilerParams(
            vmem_limit_bytes=58 << 20, dimension_semantics=("arbitrary",)
        ),
        cost_estimate=pl.CostEstimate(flops=flops, bytes_accessed=moved, transcendentals=0),
        name=name,
    )(info, *ins, *fixed_ins, *raw)


def mixer_forward(info, x, mask, gain, pieces):
    rows = x.shape[0]
    return row_call(
        mixer_forward_kernel,
        rows,
        [x, mask],
        [gain[None, :]],
        pieces,
        [(UNITED, F32), (D, BF16), (RANKS, BF16)],
        [],
        mixer_scratch(),
        info,
        "mixer_forward",
        2 * rows * D * UNITED,
        2 * D * UNITED + 4 * rows * UNITED,
    )


def block(info, joined, x, grad, mask, gain, merge_p, expand_p, reduce_p):
    rows = x.shape[0]
    return row_call(
        block_kernel,
        rows,
        [joined, x, grad, mask],
        [gain[None, :]],
        [*merge_p, *expand_p, *reduce_p],
        [(D, BF16), (DSSM, F32), (MIX - DSSM, BF16), (D, F32)],
        [(2, RANKS, GRADS_W // 2)],
        weight_scratch(MERGE)
        + weight_scratch(EXPAND)
        + weight_scratch(REDUCE)
        + [
            pltpu.VMEM((ROW_BLOCK, FF), F32),
            pltpu.VMEM((ROW_BLOCK, FF), F32),
            pltpu.VMEM((ROW_BLOCK, FF), BF16),
            pltpu.VMEM((ROW_BLOCK, 2 * FF), BF16),
            pltpu.VMEM((RANKS, GRADS_W), F32),
        ],
        info,
        "block",
        5 * rows * D * (MIX + 3 * FF),
        2 * D * (MIX + 3 * FF) + 12 * rows * D,
    )


def mixer_backward(info, grad, grad_mid, x, dmiddle, gain, pieces):
    rows = x.shape[0]
    return row_call(
        mixer_backward_kernel,
        rows,
        [grad, grad_mid, x, dmiddle],
        [gain[None, :]],
        pieces,
        [(D, BF16)],
        [],
        mixer_scratch(),
        info,
        "mixer_backward",
        2 * rows * D * UNITED,
        2 * D * UNITED + 8 * rows * D,
    )[0]


SEQ_SLOTS = 3
RANK = 16


def swap_pairs(count, bit):
    return [(i, i ^ bit) for i in range(count)]


def part_of(value, parts, place, axis=0):
    size = value.shape[axis] // parts
    return lax.dynamic_slice_in_dim(value, place * size, size, axis)


def sent_rows(weight, upper, parts, place):
    return jnp.concatenate([part_of(weight, parts, place), part_of(upper, parts, place)], axis=0)


def across(value):
    return lax.ppermute(value, "shard", swap_pairs(2, 1))


def beside(value, bit):
    return lax.ppermute(value, "rep", swap_pairs(lax.axis_size("rep"), bit))


def spread_quarter(first):
    second = beside(first, 2)
    return (first, second, beside(first, 1), beside(second, 1))


def after(value, *others):
    return lax.optimization_barrier((value, *others))[0]


def core_sums(grads):
    core = lax.axis_index("rep") % 2
    kept = lax.dynamic_index_in_dim(grads, core, 0, keepdims=False)
    sent = lax.dynamic_index_in_dim(grads, 1 - core, 0, keepdims=False).astype(BF16)
    return kept.astype(F32) + beside(sent, 1).astype(F32)


def shard_sums(total):
    side = lax.axis_index("shard")
    axis = total.ndim - 2
    mine = total.shape[axis] // 2
    kept = lax.dynamic_slice_in_dim(total, side * mine, mine, axis)
    sent = lax.dynamic_slice_in_dim(total, (1 - side) * mine, mine, axis).astype(BF16)
    return kept.astype(F32) + across(sent).astype(F32)


def all_sums(total):
    chips, shards = lax.axis_size("rep") // 2, lax.axis_size("shard")
    order = [(side, 2 * far + near) for side in range(shards) for near in range(2) for far in range(chips // 2)]
    groups = [[(2 * chip + core) * shards + side for side, chip in order] for core in range(2)]
    count = chips * shards
    parts = lax.all_to_all(
        total.astype(BF16).reshape(count, total.shape[0] // count, total.shape[1]),
        ("rep", "shard"),
        split_axis=0,
        concat_axis=0,
        axis_index_groups=groups,
        tiled=True,
    )
    return jnp.sum(parts.astype(F32), axis=0)


def far_bits():
    return [bit for bit in (4 << shift for shift in range(16)) if bit < lax.axis_size("rep")]


def swaps():
    found = [0]
    for bit in far_bits():
        found += [one + bit for one in found]
    return found[1:]


def near_sums(total):
    mine = total.shape[0] // 2
    side = lax.axis_index("rep") // 2 % 2
    kept = lax.dynamic_slice_in_dim(total, side * mine, mine, 0)
    sent = lax.dynamic_slice_in_dim(total, (1 - side) * mine, mine, 0).astype(BF16)
    return kept.astype(F32) + beside(sent, 2).astype(F32)


def far_sums(total):
    place = lax.axis_index("rep") // 4
    size = total.shape[0] // (1 + len(swaps()))
    own = lax.dynamic_slice_in_dim(total, place * size, size, 0).astype(F32)
    for swap in swaps():
        sent = lax.dynamic_slice_in_dim(total, (place ^ (swap // 4)) * size, size, 0).astype(BF16)
        own = own + beside(sent, swap).astype(F32)
    return own


def far_rows(own):
    place = lax.axis_index("rep") // 4
    parts = jnp.stack([own] + [beside(own, swap) for swap in swaps()])
    bit = 1
    while bit < parts.shape[0]:
        pairs = parts.reshape(-1, 2, bit, *own.shape)
        parts = jnp.where(place // bit % 2 == 0, pairs, pairs[:, ::-1]).reshape(-1, *own.shape)
        bit *= 2
    return parts.reshape(-1, own.shape[1])


def near_rows(own):
    other = beside(own, 2)
    return jnp.where(
        lax.axis_index("rep") // 2 % 2 == 0,
        jnp.concatenate([own, other], axis=0),
        jnp.concatenate([other, own], axis=0),
    )


def core_columns(whole):
    other = beside(whole, 1)
    return jnp.where(
        lax.axis_index("rep") % 2 == 0,
        jnp.concatenate([whole, other], axis=1),
        jnp.concatenate([other, whole], axis=1),
    )


def row_orders(assignment, stripe, groups):
    units = assignment.shape[0]
    per = units // groups
    total = stripe * units
    sending = jnp.arange(total, dtype=jnp.int32)
    row = sending // per % stripe
    chosen = jnp.broadcast_to(assignment.reshape(groups, 1, per), (groups, stripe, per))
    source = row * units + chosen.reshape(total)
    columns = jnp.arange(total, dtype=jnp.int32)
    pick = (source[:, None] == columns[None, :]).astype(BF16)
    working = jnp.arange(total, dtype=jnp.int32)
    piece, group, row = working // (groups * stripe), working // stripe % groups, working % stripe
    received = (group * stripe + row) * per + piece
    place = (received[:, None] == columns[None, :]).astype(BF16)
    return pick, place


def exchange(value):
    return lax.all_to_all(value, ("rep", "shard"), split_axis=0, concat_axis=0, tiled=True)


def on_device(
    tokens,
    cotangent,
    lengths,
    adapter_index,
    assignment,
    first_gain,
    mixer_weight,
    mixer_down,
    mixer_up,
    filter_taps,
    filter_bias,
    step_bias,
    decay_rate,
    skip_gain,
    state_gain,
    merge_weight,
    merge_down,
    merge_up,
    second_gain,
    expand_weight,
    expand_down,
    expand_up,
    reduce_weight,
    reduce_down,
    reduce_up,
):
    stripe, units, width = tokens.shape
    groups = lax.axis_size("rep") * lax.axis_size("shard")
    rows = stripe * units
    rep = lax.axis_index("rep")
    side = lax.axis_index("shard")
    quarter = rep % QUARTERS
    core = rep % 2
    info = jnp.stack(
        [side, quarter, quarter ^ 2, quarter ^ 1, quarter ^ 3, core, core ^ 1]
    ).astype(jnp.int32)

    pick, place = row_orders(assignment, stripe, groups)

    def send_rows(value):
        return dot_nn(pick, value.reshape(rows, width)).astype(BF16)

    def work_rows(value):
        return dot_nn(place, value).astype(BF16)

    def over_core(value):
        return beside(value, 1)

    def over_x(value):
        return beside(value, 2)

    mixer_t = mixer_weight.T
    mixer_sent = jnp.pad(part_of(mixer_t, QUARTERS, quarter, 1), ((0, 8), (0, 0)))
    mixer_sent = [mixer_sent[cols] for cols in MIXER_CHUNKS]
    in_one = across(mixer_sent[0])
    token_rows = exchange(send_rows(after(tokens, *mixer_sent)))

    in_two = across(after(mixer_sent[1], in_one))
    one_x = over_x(in_one)
    cotangent, lengths, merge_weight, expand_weight, reduce_weight, _ = lax.optimization_barrier(
        (cotangent, lengths, merge_weight, expand_weight, reduce_weight, in_one)
    )
    mixer_f = jnp.concatenate(
        [mixer_down, jnp.pad(mixer_up, ((0, 0), (0, UNITED - GIVEN)))], axis=1
    )
    in_f = across(after(part_of(mixer_f, QUARTERS, quarter), in_one))
    grad_sent = send_rows(cotangent)
    mixer_end = jnp.pad(mixer_t[OWN_ROWS:], ((0, OWN_ROWS + 16 - GIVEN), (0, 0)))
    block_f = jnp.concatenate([merge_down, expand_down, reduce_down], axis=1)
    merge_sent = sent_rows(merge_weight, merge_up, 4, quarter)
    expand_sent = sent_rows(expand_weight, expand_up, 4, quarter)
    expand_sent = [expand_sent[:, cols] for cols in EXPAND[4]]
    reduce_sent = sent_rows(reduce_weight, reduce_up, 2, core)
    block_f_sent = part_of(block_f, QUARTERS, quarter)

    finish = jnp.cumsum(lengths[0])
    begin = finish - lengths[0]
    blocks = jnp.arange(rows // SPAN, dtype=jnp.int32)
    member = (blocks[:, None] >= begin[None, :]) & (blocks[:, None] < finish[None, :])
    first = jnp.sum(jnp.where(member, begin[None, :], 0), axis=1).astype(jnp.int32)
    owner = jnp.sum(jnp.where(member, adapter_index[None, :], 0), axis=1)
    restart = (first == blocks).astype(jnp.int32)
    position = jnp.arange(rows, dtype=jnp.int32) - jnp.repeat(first * SPAN, SPAN)
    mask = (
        jnp.repeat(owner, SPAN)[:, None] == jnp.arange(RANKS, dtype=jnp.int32)[None, :] // RANK
    ).astype(BF16)
    cosine, sines = rotation_tables(position)
    params = ssm_params(filter_taps, filter_bias, step_bias, decay_rate, skip_gain, state_gain)

    in_two, cosine, sines, mask, *_ = lax.optimization_barrier(
        (in_two, cosine, sines, mask, mixer_end, grad_sent, merge_sent, *expand_sent, reduce_sent)
        + (block_f,)
    )

    two_x = over_x(in_two)
    merge_in = across(after(merge_sent, in_two))
    expand_one = across(after(expand_sent[0], in_two))
    in_f = after(in_f, in_two)
    f_x = over_x(in_f)
    one_x, two_x, f_x, merge_in = lax.optimization_barrier((one_x, two_x, f_x, merge_in))
    mixer_f_p = (mixer_f, in_f, f_x, over_core(in_f), over_core(f_x))
    mixer_p = (
        *mixer_f_p,
        mixer_t,
        mixer_end,
        in_one,
        one_x,
        over_core(in_one),
        over_core(one_x),
        in_two,
        two_x,
        over_core(in_two),
        over_core(two_x),
    )
    grad_rows = exchange(after(grad_sent, token_rows))
    x = work_rows(token_rows)

    gate = merge_in
    block_f_in = across(after(block_f_sent, gate))
    merge_x = over_x(merge_in)
    expand_two = across(after(expand_sent[1], gate))
    united, hidden, mixer_mid = mixer_forward(info, x, mask, first_gain, mixer_p)
    united, block_f_in, expand_one = lax.optimization_barrier((united, block_f_in, expand_one))

    reduce_in = across(after(reduce_sent, united))
    expand_one_x = over_x(expand_one)
    block_f_x = over_x(block_f_in)
    attended, logs, turned, kv_low = attend_forward(united, cosine, sines, first)
    attended, merge_x, expand_two = lax.optimization_barrier((attended, merge_x, expand_two))

    expand_two_x = over_x(expand_two)
    near = [over_core(v) for v in (merge_in, merge_x, expand_one, expand_two, block_f_in)]
    joined, scan, starts = mamba_forward(united, attended, restart, params)
    joined, reduce_in, expand_one_x, expand_two_x, block_f_x, *near = lax.optimization_barrier(
        (joined, reduce_in, expand_one_x, expand_two_x, block_f_x, *near)
    )

    merge_c, merge_xc, expand_one_c, expand_two_c, block_f_c = near
    lowers = (block_f, block_f_in, block_f_x, block_f_c, over_core(block_f_x))
    merge_p = (*lowers, merge_weight, merge_up, merge_in, merge_x, merge_c, merge_xc)
    expand_p = (
        *lowers,
        expand_weight,
        expand_up,
        expand_one,
        expand_one_x,
        expand_one_c,
        over_core(expand_one_x),
        expand_two,
        expand_two_x,
        expand_two_c,
        over_core(expand_two_x),
    )
    reduce_p = (*lowers, reduce_weight, reduce_up, reduce_in, over_core(reduce_in))
    grad_top = work_rows(after(grad_rows, joined))
    mixed, dmamba, dattended, dmiddle, block_grads = block(
        info, joined, x, grad_top, mask, second_gain, merge_p, expand_p, reduce_p
    )

    def leaving(value):
        return lax.dot_general(
            place, value, (((0,), (0,)), ((), ())), preferred_element_type=F32
        ).astype(BF16)

    def input_rows(value, kind):
        return (
            lax.dot_general(pick, value, (((0,), (0,)), ((), ())), preferred_element_type=F32)
            .astype(kind)
            .reshape(stripe, units, width)
        )

    block_sums = core_sums(block_grads)
    dattended, block_sums, mixed = lax.optimization_barrier((dattended, block_sums, mixed))
    block_sums = shard_sums(block_sums)
    mixed_leaving = leaving(mixed)
    dquery, dkv = attend_backward(turned, kv_low, dattended, logs, cosine, sines, first)
    dquery, block_sums, mixed_leaving = lax.optimization_barrier(
        (dquery, block_sums, mixed_leaving)
    )
    mixed_rows = exchange(mixed_leaving)
    block_sums = near_sums(block_sums)
    dunited, grad_mid, mixer_grads = mamba_backward(
        united, scan, starts, dmamba, dquery, dkv, hidden, mixer_mid, mask, restart, info, params,
        mixer_f_p,
    )
    dunited, block_sums, mixed_rows, mixer_grads = lax.optimization_barrier(
        (dunited, block_sums, mixed_rows, mixer_grads)
    )
    mixer_sums = core_sums(mixer_grads)
    dunited, mixer_sums = lax.optimization_barrier((dunited, mixer_sums))
    mixer_sums = all_sums(mixer_sums)
    block_sums = far_sums(block_sums)
    work_grad = mixer_backward(info, dunited, grad_mid, x, dmiddle, first_gain, mixer_p)
    work_grad, block_sums, mixer_sums = lax.optimization_barrier(
        (work_grad, block_sums, mixer_sums)
    )
    grad_leaving = leaving(work_grad)
    token_grads = exchange(grad_leaving)
    mixer_sums, block_sums, mixed_rows, _ = lax.optimization_barrier(
        (mixer_sums, block_sums, mixed_rows, grad_leaving)
    )

    def finish(_, carry):
        mixer_sums, block_sums, _ = carry
        sums = jnp.concatenate([mixer_sums, block_sums], axis=1)
        return mixer_sums, block_sums, core_columns(near_rows(far_rows(sums.astype(BF16))))

    cut = mixer_sums.shape[1]
    _, _, final = lax.fori_loop(
        0,
        lax.optimization_barrier(jnp.int32(1)),
        finish,
        (
            mixer_sums,
            block_sums,
            jnp.zeros((RANKS // 2, 2 * (cut + block_sums.shape[1])), BF16),
        ),
    )
    final = final.reshape(RANKS // 2, 2, -1)
    mixer_final = final[:, :, :cut].reshape(RANKS // 2, -1).astype(F32)
    block_final = final[:, :, cut:].reshape(RANKS // 2, -1).astype(F32)
    mixed_out = input_rows(mixed_rows, BF16)
    return (
        mixed_out,
        input_rows(token_grads, F32),
        mixer_final[:, :D],
        mixer_final[:, D : D + GIVEN],
        block_final[:, MERGE_L],
        block_final[:, MERGE_U],
        block_final[:, EXPAND_L],
        block_final[:, EXPAND_U],
        block_final[:, REDUCE_L],
        block_final[:, REDUCE_U],
    )


def solution(mesh):
    split = ("rep", "shard")
    sharded = P("shard", None)
    placed = (
        P(split, None, None),
        P(split, None, None),
        P(split, None),
        P(split),
        P(),
        P(),
        sharded,
        sharded,
        sharded,
        P(),
        P(),
        P(),
        P(),
        P(),
        P(),
        sharded,
        sharded,
        sharded,
        P(),
        sharded,
        sharded,
        sharded,
        sharded,
        sharded,
        sharded,
    )
    return jax.shard_map(
        on_device,
        mesh=mesh,
        in_specs=placed,
        out_specs=(P(split, None, None), P(split, None, None)) + (sharded,) * 8,
        check_vma=False,
    )
```
